32 devices in a mesh: grp: 8 (over z, x), sp: 4 (over y, core).
Axes of the slice: x: 2, y: 2, z: 4, core: 2. Of those that a mesh axis runs over, the one named last changes fastest.
Arguments:
- queries: bfloat16 [8, 768, 2048], P('grp', 'sp'), may hold values from -15 to 15
- keys: bfloat16 [8, 768, 2048], P('grp', 'sp'), may hold values from -6 to 6
- values: bfloat16 [8, 768, 2048], P('grp', 'sp'), may hold values from -6 to 6
- ref_cache: bfloat16 [8, 2, 512, 2048], P('grp', None, 'sp'), may hold values from -6 to 6
- ref_ids: int32 [8], replicated, may hold values from 0 to 7
- ref_owner: int32 [8], replicated, may hold values from 0 to 7, each once
- ref_lens: int32 [8], replicated, may hold values from 64 to 512, as said below
Outputs:
- attended: bfloat16 [8, 768, 2048], P('grp', 'sp')
The draws below stay inside these ranges and needn't reach their ends.
Inputs may be any that keep to these rules, and one draw needn't show every extreme that they name: `ref_owner`: each reference image lies in exactly one cache row. `ref_lens`: some reference has 512 live tokens and some 512 // 8.
All inputs are finite; a program needn't handle non-finite values.
Results may differ from the reference program's by a relative error of at most 0.0031.
Values may be sent and summed in bfloat16 or wider, within the bound.
A program may use at most 64 MiB of HBM per device.

```python
import math
import jax
import jax.numpy as jnp
import numpy as np
from jax import lax

HEADS = 16
HEAD_DIM = 128
ATTN_WIDTH = 2048
SEQ = 768
REF_LEN = 512
N_GRP = 8


def draw_queries(key, part):
    key = jax.random.fold_in(key, 11)
    shape_all = (N_GRP, SEQ, HEADS * HEAD_DIM)
    base = jnp.clip(2.5 * jax.random.normal(key, shape_all, jnp.float32), -15.0, 15.0)
    return base.astype(jnp.bfloat16)


def draw_keys(key, part):
    key = jax.random.fold_in(key, 12)
    shape_all = (N_GRP, SEQ, HEADS * HEAD_DIM)
    base = jnp.clip(jax.random.normal(key, shape_all, jnp.float32), -6.0, 6.0)
    return base.astype(jnp.bfloat16)


def draw_ref_lens(key, part):
    key = jax.random.fold_in(key, 13)
    first_key, second_key = jax.random.split(key)
    lengths = jax.random.randint(first_key, (N_GRP,), REF_LEN // 8, REF_LEN + 1)
    order = jax.random.permutation(second_key, N_GRP)
    lengths = lengths.at[order[0]].set(REF_LEN).at[order[1]].set(REF_LEN // 8)
    return lengths.astype(jnp.int32)


def place_ends(result, rng, least, top_value):
    dims = result.shape
    place = [jax.random.randint(jax.random.fold_in(rng, axis), (), 0, dims[axis]) for axis in range(len(dims))]
    result = result.at[tuple(place)].set(least)
    longest = dims.index(max(dims))
    place[longest] = (place[longest] + 1) % dims[longest]
    return result.at[tuple(place)].set(top_value)


def steps_of(key, dims, pieces, least, largest):
    level, own = 1.0, jax.random.fold_in(key, 6)
    for position, blocks in pieces:
        heights = jnp.exp(jax.random.uniform(jax.random.fold_in(own, position), (blocks,), jnp.float32, least / len(pieces), largest / len(pieces)))
        level = level * jnp.repeat(heights, dims[position] // blocks).reshape([-1 if axis == position else 1 for axis in range(len(dims))])
    return level


def cumulative_ranks(number_of, skew):
    weights = [(1 << 20) // math.isqrt(grade ** skew) + 1 for grade in range(1, number_of + 1)]
    deviation = 1 + sum(weights) // (1 << 30)
    return np.cumsum(np.array([max(1, weight // deviation) for weight in weights]))


def ranked_ids(key, dims, count, slope):
    grid = cumulative_ranks(count, slope)
    ticket = jax.random.randint(jax.random.fold_in(key, 1), dims, 0, int(grid[count - 1]))
    rank = jnp.searchsorted(jnp.asarray(grid, jnp.int32), ticket, side="right")
    return jax.random.permutation(jax.random.fold_in(key, 2), count)[rank].astype(jnp.int32)


def scatter_about(own_key, shape, deviation, most, cuts=(), kind=jnp.bfloat16):
    entries = deviation * jax.random.normal(own_key, shape, jnp.float32)
    if cuts:
        entries = entries * steps_of(own_key, shape, cuts, -0.22, 0.18)
    return jnp.clip(entries, -most, most).astype(kind)


def setup_inputs(seed: int = 0) -> dict:
    streams_of = jax.random.split(jax.random.key(seed), 8)
    queries = draw_queries(jax.random.fold_in(streams_of[7], 71), 0)
    keys = draw_keys(jax.random.fold_in(streams_of[7], 71), 0)
    values = scatter_about(streams_of[2], (N_GRP, SEQ, ATTN_WIDTH), 1.0, 6.0, ((0, 8), (1, 4)))
    ref_cache = scatter_about(streams_of[3], (N_GRP, 2, REF_LEN, ATTN_WIDTH), 1.0, 6.0, ((0, 8), (2, 4)))
    ref_ids = place_ends(ranked_ids(streams_of[4], (N_GRP,), N_GRP, 2), jax.random.fold_in(streams_of[4], 3), 0, N_GRP - 1).astype(jnp.int32)
    ref_owner = jax.random.permutation(streams_of[5], N_GRP).astype(jnp.int32)
    ref_lens = draw_ref_lens(jax.random.fold_in(streams_of[7], 71), 0)
    return {"queries": queries, "keys": keys, "values": values, "ref_cache": ref_cache, "ref_ids": ref_ids, "ref_owner": ref_owner, "ref_lens": ref_lens}


def reference(queries, keys, values, ref_cache, ref_ids, ref_owner, ref_lens):
    wanted_row = ref_owner[ref_ids].astype(jnp.int32)
    ref_live = ref_lens[ref_ids].astype(jnp.int32)
    score_scale = HEAD_DIM ** -0.5

    def one_group(group_idx):
        cache_row = lax.dynamic_index_in_dim(ref_cache, wanted_row[group_idx], 0, keepdims=False)
        key_set = jnp.concatenate([keys[group_idx], cache_row[0]], axis=0)
        value_set = jnp.concatenate([values[group_idx], cache_row[1]], axis=0)
        live_mask = jnp.arange(SEQ + REF_LEN, dtype=jnp.int32) < SEQ + ref_live[group_idx]
        own_queries = queries[group_idx]

        def one_head(head_idx):
            start = (head_idx * HEAD_DIM).astype(jnp.int32)
            q_head = lax.dynamic_slice_in_dim(own_queries, start, HEAD_DIM, 1)
            k_head = lax.dynamic_slice_in_dim(key_set, start, HEAD_DIM, 1)
            v_head = lax.dynamic_slice_in_dim(value_set, start, HEAD_DIM, 1)
            scores = jnp.dot(q_head, k_head.T, preferred_element_type=jnp.float32) * score_scale
            scores = jnp.where(live_mask[None, :], scores, -jnp.inf)
            row_peak = jnp.max(scores, axis=-1, keepdims=True)
            weights = jnp.exp(scores - row_peak)
            row_total = jnp.sum(weights, axis=-1, keepdims=True)
            soft_probs = weights.astype(jnp.bfloat16)
            mixed_out = jnp.dot(soft_probs, v_head, preferred_element_type=jnp.float32)
            return (mixed_out / row_total).astype(jnp.bfloat16)

        head_outs = lax.map(one_head, jnp.arange(HEADS, dtype=jnp.int32))
        return jnp.transpose(head_outs, (1, 0, 2)).reshape(SEQ, HEADS * HEAD_DIM)

    return lax.map(one_group, jnp.arange(N_GRP, dtype=jnp.int32))
```

```python
import functools

import jax
import jax.numpy as jnp
from jax import lax
from jax.experimental import pallas as pl
from jax.experimental.pallas import tpu as pltpu
from jax.sharding import PartitionSpec as P

HEAD_DIM = 128
PAIR = 2
MESH = pl.DeviceIdType.MESH


def slots_on(p, levels):
    return min(PAIR * (p + 1), levels - 1 - p)


def sends_rows(p, levels):
    return PAIR * (p + 1) <= levels - 1 - p


def pick(options):
    value = options[-1][1]
    for cond, other in reversed(options[:-1]):
        value = lax.select(cond, other, value)
    return value


def kernel(
    n_grp, n_sp,
    ids_ref, owner_ref, lens_ref, q_hbm, k_hbm, v_hbm, ref_hbm, out_hbm,
    q_buf, k_buf, v_buf, own_buf, x_buf, line_in, line_out, routed, ref_kv, o_buf,
    own_sem, keep_sem, seq_send, seq_recv, x_send, x_recv, line_send, line_recv,
    ref_send, ref_recv, o_keep, o_send, o_recv,
):
    levels = n_grp // PAIR
    heads = ref_hbm.shape[-1] // HEAD_DIM
    per_dev = heads // n_sp
    feat = per_dev * HEAD_DIM
    tokens = q_hbm.shape[1]
    ref_tokens = ref_hbm.shape[2]
    grp = lax.axis_index("grp")
    sp = lax.axis_index("sp")
    level = grp // PAIR
    side = grp % PAIR
    mate = level * PAIR + (1 - side)

    def at_level(other):
        return (other * PAIR + side, sp)

    barrier = pltpu.get_barrier_semaphore()

    def greet(device):
        pl.semaphore_signal(barrier, inc=1, device_id=device, device_id_type=MESH)

    greet((mate, sp))
    for step in range(1, n_sp):
        greet((grp, (sp + step) % n_sp))

    @pl.when(level > 0)
    def _():
        greet(at_level(level - 1))

    @pl.when(level < levels - 1)
    def _():
        greet(at_level(level + 1))

    inner = jnp.logical_and(level > 0, level < levels - 1)
    pl.semaphore_wait(barrier, n_sp + 1 + inner.astype(jnp.int32))

    def head_of(c):
        return (c + sp) % n_sp, c // n_sp

    def lanes_of(c):
        dest, local = head_of(c)
        return pl.ds(pl.multiple_of((dest * per_dev + local) * HEAD_DIM, HEAD_DIM), HEAD_DIM)

    def own_copy(c):
        return pltpu.make_async_copy(
            ref_hbm.at[0, :, :, lanes_of(c)], own_buf.at[c], own_sem.at[c]
        )

    def x_copy(c):
        return pltpu.make_async_remote_copy(
            src_ref=ref_hbm.at[0, :, :, lanes_of(c)], dst_ref=x_buf.at[c],
            send_sem=x_send.at[c], recv_sem=x_recv.at[c],
            device_id=(mate, sp), device_id_type=MESH,
        )

    def line_copy(way, slot, c, src, other):
        return pltpu.make_async_remote_copy(
            src_ref=src, dst_ref=line_in.at[way, slot, c],
            send_sem=line_send.at[way, slot, c], recv_sem=line_recv.at[way, slot, c],
            device_id=at_level(other), device_id_type=MESH,
        )

    def ref_copy(c, dest, local, src):
        return pltpu.make_async_remote_copy(
            src_ref=routed.at[c], dst_ref=ref_kv.at[local, src],
            send_sem=ref_send.at[c], recv_sem=ref_recv.at[local, src],
            device_id=(grp, dest), device_id_type=MESH,
        )

    seq_pairs = ((q_hbm, q_buf), (k_hbm, k_buf), (v_hbm, v_buf))

    def seq_lanes(dest):
        return pl.ds(pl.multiple_of(dest * feat, HEAD_DIM), feat)

    def seq_copy(a, dest, src):
        hbm, buf = seq_pairs[a]
        return pltpu.make_async_remote_copy(
            src_ref=hbm.at[0, :, seq_lanes(dest)], dst_ref=buf.at[src],
            send_sem=seq_send.at[a, dest], recv_sem=seq_recv.at[a, src],
            device_id=(grp, dest), device_id_type=MESH,
        )

    def keep_copy(a):
        hbm, buf = seq_pairs[a]
        return pltpu.make_async_copy(
            hbm.at[0, :, seq_lanes(sp)], buf.at[sp], keep_sem.at[a]
        )

    def o_copy(local, dest, src):
        lanes = pl.ds(pl.multiple_of(local * HEAD_DIM, HEAD_DIM), HEAD_DIM)
        out_lanes = pl.ds(pl.multiple_of(src * feat + local * HEAD_DIM, HEAD_DIM), HEAD_DIM)
        return pltpu.make_async_remote_copy(
            src_ref=o_buf.at[dest, :, lanes], dst_ref=out_hbm.at[0, :, out_lanes],
            send_sem=o_send.at[local, dest], recv_sem=o_recv.at[local, src],
            device_id=(grp, dest), device_id_type=MESH,
        )

    def o_here(local):
        lanes = pl.ds(pl.multiple_of(local * HEAD_DIM, HEAD_DIM), HEAD_DIM)
        out_lanes = pl.ds(pl.multiple_of(sp * feat + local * HEAD_DIM, HEAD_DIM), HEAD_DIM)
        return pltpu.make_async_copy(
            o_buf.at[sp, :, lanes], out_hbm.at[0, :, out_lanes], o_keep.at[local]
        )

    def loop(count, body):
        def step(i, carry):
            body(i)
            return carry
        lax.fori_loop(0, count, step, 0)

    @functools.partial(loop, heads)
    def _(c):
        x_copy(c).start()
        own_copy(c).start()

    @functools.partial(loop, n_sp - 1)
    def _(step):
        dest = (sp + 1 + step) % n_sp
        for a in range(3):
            seq_copy(a, dest, sp).start()

    for a in range(3):
        keep_copy(a).start()

    @functools.partial(loop, heads)
    def _(c):
        own_copy(c).wait()

    wanted = [owner_ref[ids_ref[lev * PAIR + side]] for lev in range(levels)]
    here = ids_ref[grp]
    my_row = owner_ref[here]
    live = lens_ref[here]

    def level_rows(c):
        own, other = own_buf[c], x_buf[c]
        return [lax.select(side == k, own, other) for k in range(PAIR)]

    for at, way in ((0, 0), (levels - 1, 1)):
        @pl.when(level == at)
        def _(at=at, way=way):
            ahead = at + 1 if way == 0 else at - 1

            @functools.partial(loop, heads)
            def _(c):
                line_copy(way, side, c, own_buf.at[c], ahead).start()
                x_copy(c).wait_recv()
                line_copy(way, 1 - side, c, x_buf.at[c], ahead).start()

    def place(way, lev):
        return lev if way == 0 else levels - 1 - lev

    def relay(at, way, c):
        p = place(way, at)
        ahead = at + 1 if way == 0 else at - 1
        for slot in range(slots_on(p - 1, levels)):
            line_copy(way, slot, c, x_buf.at[c], at).wait_recv()
        if p == levels - 1:
            return
        count = slots_on(p, levels)
        if sends_rows(p, levels):
            for slot in range(PAIR * p):
                line_copy(way, slot, c, line_in.at[way, slot, c], ahead).start()
            line_copy(way, PAIR * p + side, c, own_buf.at[c], ahead).start()
            line_copy(way, PAIR * p + 1 - side, c, x_buf.at[c], ahead).start()
            return
        rows = level_rows(c)
        for slot in range(count):
            row = wanted[place(way, p + 1 + slot)]
            value = pick(line_options(at, way, c, row, slot + 1, rows))
            line_out[way, slot, c] = value
            line_copy(way, slot, c, line_out.at[way, slot, c], ahead).start()

    def line_options(at, way, c, row, slot, rows):
        p = place(way, at)
        options = [(row == at * PAIR + k, rows[k]) for k in range(PAIR)]
        if p == 0:
            return options
        if sends_rows(p - 1, levels):
            return options + [
                (row == place(way, q) * PAIR + k, line_in[way, PAIR * q + k, c])
                for q in range(p) for k in range(PAIR)
            ]
        return options + [(row // PAIR < at if way == 0 else row // PAIR > at, line_in[way, slot, c])]

    def final(at, c):
        rows = level_rows(c)
        options = line_options(at, 0, c, my_row, 0, rows)
        options = options + line_options(at, 1, c, my_row, 0, rows)[PAIR:]
        value = pick(options)
        dest, local = head_of(c)

        @pl.when(dest == sp)
        def _():
            ref_kv[local, sp] = value

        @pl.when(dest != sp)
        def _():
            routed[c] = value
            ref_copy(c, dest, local, sp).start()

    def attend(local, block):
        lanes = pl.ds(pl.multiple_of(local * HEAD_DIM, HEAD_DIM), HEAD_DIM)
        own_keys, ref_keys = n_sp * tokens, n_sp * ref_tokens
        q = q_buf[block, :, lanes]
        k = k_buf[:, :, lanes].reshape(own_keys, HEAD_DIM)
        v = v_buf[:, :, lanes].reshape(own_keys, HEAD_DIM)
        ref_k = ref_kv[local, :, 0].reshape(ref_keys, HEAD_DIM)
        ref_v = ref_kv[local, :, 1].reshape(ref_keys, HEAD_DIM)
        contract = (((1,), (1,)), ((), ()))
        scale = HEAD_DIM ** -0.5
        s_own = lax.dot_general(q, k, contract, preferred_element_type=jnp.float32) * scale
        s_ref = lax.dot_general(q, ref_k, contract, preferred_element_type=jnp.float32) * scale
        col = lax.broadcasted_iota(jnp.int32, s_ref.shape, 1)
        s_ref = jnp.where(col < live, s_ref, -jnp.inf)
        peak = jnp.maximum(
            jnp.max(s_own, axis=1, keepdims=True), jnp.max(s_ref, axis=1, keepdims=True)
        )
        w_own = jnp.exp(s_own - peak)
        w_ref = jnp.exp(s_ref - peak)
        total = jnp.sum(w_own, axis=1, keepdims=True) + jnp.sum(w_ref, axis=1, keepdims=True)
        mixed = jnp.dot(w_own.astype(jnp.bfloat16), v, preferred_element_type=jnp.float32)
        mixed += jnp.dot(w_ref.astype(jnp.bfloat16), ref_v, preferred_element_type=jnp.float32)
        o_buf[block, :, lanes] = (mixed / total).astype(jnp.bfloat16)

    last_lag = levels - 2
    first_unit = max(n_sp - 1 + last_lag, 3 * heads // 4)
    units = per_dev * n_sp

    @functools.partial(loop, max(heads + last_lag, first_unit + units))
    def _(i):
        @pl.when(jnp.logical_and(inner, i < heads))
        def _():
            x_copy(i).wait_recv()

        for at in range(levels):
            @pl.when(level == at)
            def _(at=at):
                for way in (0, 1):
                    p = place(way, at)
                    if p == 0:
                        continue
                    c = i - (p - 1)

                    @pl.when(jnp.logical_and(c >= 0, c < heads))
                    def _(c=c, way=way):
                        relay(at, way, c)

                done = i - last_lag

                @pl.when(jnp.logical_and(done >= 0, done < heads))
                def _():
                    final(at, done)

        unit = i - first_unit

        @pl.when(jnp.logical_and(unit >= 0, unit < units))
        def _():
            local, turn = unit // n_sp, unit % n_sp
            block = (sp + 1 + turn) % n_sp

            @pl.when(unit == 0)
            def _():
                for a in range(3):
                    keep_copy(a).wait()

                @functools.partial(loop, n_sp - 1)
                def _(step):
                    src = (sp + 1 + step) % n_sp
                    for a in range(3):
                        seq_copy(a, sp, src).wait_recv()

            @pl.when(turn == 0)
            def _():
                @functools.partial(loop, n_sp - 1)
                def _(step):
                    src = (sp + 1 + step) % n_sp
                    ref_copy(0, sp, local, src).wait_recv()

            attend(local, block)

            @pl.when(block == sp)
            def _():
                o_here(local).start()

            @pl.when(block != sp)
            def _():
                o_copy(local, block, sp).start()

    @functools.partial(loop, heads)
    def _(c):
        x_copy(c).wait_send()
        dest, local = head_of(c)

        @pl.when(dest != sp)
        def _():
            ref_copy(c, dest, local, sp).wait_send()

        for at in range(levels):
            @pl.when(level == at)
            def _(at=at):
                for way in (0, 1):
                    p = place(way, at)
                    if p < levels - 1:
                        for slot in range(slots_on(p, levels)):
                            line_copy(way, slot, c, x_buf.at[c], at).wait_send()

    @functools.partial(loop, n_sp - 1)
    def _(step):
        other = (sp + 1 + step) % n_sp
        for a in range(3):
            seq_copy(a, other, sp).wait_send()
        for local in range(per_dev):
            o_copy(local, other, sp).wait_send()
            o_copy(local, sp, other).wait_recv()

    for local in range(per_dev):
        o_here(local).wait()


def shards(n_grp, n_sp, queries, keys, values, ref_cache, ref_ids, ref_owner, ref_lens):
    tokens, width = queries.shape[1:]
    ref_tokens = ref_cache.shape[2]
    heads = width // HEAD_DIM
    per_dev = heads // n_sp
    feat = per_dev * HEAD_DIM
    levels = n_grp // PAIR
    slots = max(slots_on(p, levels) for p in range(levels - 1))
    chunk = (2, ref_tokens, HEAD_DIM)
    bf16 = jnp.bfloat16
    dma = pltpu.SemaphoreType.DMA
    smem = pl.BlockSpec(memory_space=pltpu.SMEM)
    hbm = pl.BlockSpec(memory_space=pl.ANY)
    all_keys = n_sp * (tokens + ref_tokens)
    return pl.pallas_call(
        functools.partial(kernel, n_grp, n_sp),
        out_shape=jax.ShapeDtypeStruct(queries.shape, bf16),
        in_specs=[smem] * 3 + [hbm] * 4,
        out_specs=hbm,
        scratch_shapes=[
            pltpu.VMEM((n_sp, tokens, feat), bf16),
            pltpu.VMEM((n_sp, tokens, feat), bf16),
            pltpu.VMEM((n_sp, tokens, feat), bf16),
            pltpu.VMEM((heads,) + chunk, bf16),
            pltpu.VMEM((heads,) + chunk, bf16),
            pltpu.VMEM((2, slots, heads) + chunk, bf16),
            pltpu.VMEM((2, slots, heads) + chunk, bf16),
            pltpu.VMEM((heads,) + chunk, bf16),
            pltpu.VMEM((per_dev, n_sp) + chunk, bf16),
            pltpu.VMEM((n_sp, tokens, feat), bf16),
            dma((heads,)),
            dma((3,)),
            dma((3, n_sp)),
            dma((3, n_sp)),
            dma((heads,)),
            dma((heads,)),
            dma((2, slots, heads)),
            dma((2, slots, heads)),
            dma((heads,)),
            dma((per_dev, n_sp)),
            dma((per_dev,)),
            dma((per_dev, n_sp)),
            dma((per_dev, n_sp)),
        ],
        compiler_params=pltpu.CompilerParams(
            collective_id=0, has_side_effects=True, vmem_limit_bytes=60 * 1024 * 1024
        ),
        cost_estimate=pl.CostEstimate(
            flops=4 * n_sp * tokens * all_keys * feat,
            bytes_accessed=8 * tokens * width * 2,
            transcendentals=per_dev * n_sp * tokens * all_keys,
        ),
    )(ref_ids, ref_owner, ref_lens, queries, keys, values, ref_cache)


def solution(mesh):
    in_specs = (
        P("grp", "sp", None),
        P("grp", "sp", None),
        P("grp", "sp", None),
        P("grp", None, "sp", None),
        P(),
        P(),
        P(),
    )
    body = functools.partial(shards, mesh.shape["grp"], mesh.shape["sp"])
    return jax.shard_map(
        body, mesh=mesh, in_specs=in_specs, out_specs=P("grp", "sp", None), check_vma=False
    )
```

```python
import functools

import jax
import jax.numpy as jnp
from jax import lax
from jax.experimental import pallas as pl
from jax.experimental.pallas import tpu as pltpu
from jax.sharding import PartitionSpec as P

HEAD_DIM = 128
PAIR = 2
MESH = pl.DeviceIdType.MESH


def slots_on(p, levels):
    return min(PAIR * (p + 1), levels - 1 - p)


def sends_rows(p, levels):
    return PAIR * (p + 1) <= levels - 1 - p


def pick(options):
    value = options[-1][1]
    for cond, other in reversed(options[:-1]):
        value = lax.select(cond, other, value)
    return value


def kernel(
    n_grp, n_sp,
    ids_ref, owner_ref, lens_ref, q_hbm, k_hbm, v_hbm, ref_hbm, out_hbm,
    q_buf, k_buf, v_buf, own_buf, x_buf, line_in, line_out, routed, ref_kv, o_buf,
    own_sem, keep_sem, seq_send, seq_recv, x_send, x_recv, line_send, line_recv,
    ref_send, ref_recv, o_keep, o_send, o_recv,
):
    levels = n_grp // PAIR
    heads = ref_hbm.shape[-1] // HEAD_DIM
    per_dev = heads // n_sp
    feat = per_dev * HEAD_DIM
    tokens = q_hbm.shape[1]
    ref_tokens = ref_hbm.shape[2]
    grp = lax.axis_index("grp")
    sp = lax.axis_index("sp")
    level = grp // PAIR
    side = grp % PAIR
    mate = level * PAIR + (1 - side)

    def at_level(other):
        return (other * PAIR + side, sp)

    barrier = pltpu.get_barrier_semaphore()

    def greet(device):
        pl.semaphore_signal(barrier, inc=1, device_id=device, device_id_type=MESH)

    greet((mate, sp))
    for step in range(1, n_sp):
        greet((grp, (sp + step) % n_sp))

    @pl.when(level > 0)
    def _():
        greet(at_level(level - 1))

    @pl.when(level < levels - 1)
    def _():
        greet(at_level(level + 1))

    inner = jnp.logical_and(level > 0, level < levels - 1)
    pl.semaphore_wait(barrier, n_sp + 1 + inner.astype(jnp.int32))

    def head_of(c):
        return (c + sp) % n_sp, c // n_sp

    def lanes_of(c):
        dest, local = head_of(c)
        return pl.ds(pl.multiple_of((dest * per_dev + local) * HEAD_DIM, HEAD_DIM), HEAD_DIM)

    def own_copy(c):
        return pltpu.make_async_copy(
            ref_hbm.at[0, :, :, lanes_of(c)], own_buf.at[c], own_sem.at[c]
        )

    def x_copy(c):
        return pltpu.make_async_remote_copy(
            src_ref=ref_hbm.at[0, :, :, lanes_of(c)], dst_ref=x_buf.at[c],
            send_sem=x_send.at[c], recv_sem=x_recv.at[c],
            device_id=(mate, sp), device_id_type=MESH,
        )

    def line_copy(way, slot, c, src, other):
        return pltpu.make_async_remote_copy(
            src_ref=src, dst_ref=line_in.at[way, slot, c],
            send_sem=line_send.at[way, slot, c], recv_sem=line_recv.at[way, slot, c],
            device_id=at_level(other), device_id_type=MESH,
        )

    def ref_copy(c, dest, local, src):
        return pltpu.make_async_remote_copy(
            src_ref=routed.at[c], dst_ref=ref_kv.at[local, src],
            send_sem=ref_send.at[c], recv_sem=ref_recv.at[local, src],
            device_id=(grp, dest), device_id_type=MESH,
        )

    seq_pairs = ((q_hbm, q_buf), (k_hbm, k_buf), (v_hbm, v_buf))

    def seq_lanes(dest):
        return pl.ds(pl.multiple_of(dest * feat, HEAD_DIM), feat)

    def seq_copy(a, dest, src):
        hbm, buf = seq_pairs[a]
        return pltpu.make_async_remote_copy(
            src_ref=hbm.at[0, :, seq_lanes(dest)], dst_ref=buf.at[src],
            send_sem=seq_send.at[a, dest], recv_sem=seq_recv.at[a, src],
            device_id=(grp, dest), device_id_type=MESH,
        )

    def keep_copy(a):
        hbm, buf = seq_pairs[a]
        return pltpu.make_async_copy(
            hbm.at[0, :, seq_lanes(sp)], buf.at[sp], keep_sem.at[a]
        )

    def o_copy(local, dest, src):
        lanes = pl.ds(pl.multiple_of(local * HEAD_DIM, HEAD_DIM), HEAD_DIM)
        out_lanes = pl.ds(pl.multiple_of(src * feat + local * HEAD_DIM, HEAD_DIM), HEAD_DIM)
        return pltpu.make_async_remote_copy(
            src_ref=o_buf.at[dest, :, lanes], dst_ref=out_hbm.at[0, :, out_lanes],
            send_sem=o_send.at[local, dest], recv_sem=o_recv.at[local, src],
            device_id=(grp, dest), device_id_type=MESH,
        )

    def o_here(local):
        lanes = pl.ds(pl.multiple_of(local * HEAD_DIM, HEAD_DIM), HEAD_DIM)
        out_lanes = pl.ds(pl.multiple_of(sp * feat + local * HEAD_DIM, HEAD_DIM), HEAD_DIM)
        return pltpu.make_async_copy(
            o_buf.at[sp, :, lanes], out_hbm.at[0, :, out_lanes], o_keep.at[local]
        )

    def loop(count, body):
        def step(i, carry):
            body(i)
            return carry
        lax.fori_loop(0, count, step, 0)

    x_ahead, ends_ahead = 5, 3
    seq_copies = 3 * (n_sp - 1)
    per_step = -(-seq_copies // 9)

    @functools.partial(loop, x_ahead)
    def _(c):
        x_copy(c).start()

    @functools.partial(loop, heads)
    def _(c):
        own_copy(c).start()

    for a in range(3):
        keep_copy(a).start()

    @functools.partial(loop, heads)
    def _(c):
        own_copy(c).wait()

    wanted = [owner_ref[ids_ref[lev * PAIR + side]] for lev in range(levels)]
    here = ids_ref[grp]
    my_row = owner_ref[here]
    live = lens_ref[here]

    def level_rows(c):
        own, other = own_buf[c], x_buf[c]
        return [lax.select(side == k, own, other) for k in range(PAIR)]

    def send_rows(at, c):
        way, ahead = (0, at + 1) if at == 0 else (1, at - 1)
        line_copy(way, side, c, own_buf.at[c], ahead).start()
        x_copy(c).wait_recv()
        line_copy(way, 1 - side, c, x_buf.at[c], ahead).start()

    for at in (0, levels - 1):
        @pl.when(level == at)
        def _(at=at):
            @functools.partial(loop, ends_ahead)
            def _(c):
                send_rows(at, c)

    def place(way, lev):
        return lev if way == 0 else levels - 1 - lev

    def relay(at, way, c):
        p = place(way, at)
        ahead = at + 1 if way == 0 else at - 1
        for slot in range(slots_on(p - 1, levels)):
            line_copy(way, slot, c, x_buf.at[c], at).wait_recv()
        if p == levels - 1:
            return
        count = slots_on(p, levels)
        if sends_rows(p, levels):
            for slot in range(PAIR * p):
                line_copy(way, slot, c, line_in.at[way, slot, c], ahead).start()
            line_copy(way, PAIR * p + side, c, own_buf.at[c], ahead).start()
            line_copy(way, PAIR * p + 1 - side, c, x_buf.at[c], ahead).start()
            return
        rows = level_rows(c)
        for slot in range(count):
            row = wanted[place(way, p + 1 + slot)]
            value = pick(line_options(at, way, c, row, slot + 1, rows))
            line_out[way, slot, c] = value
            line_copy(way, slot, c, line_out.at[way, slot, c], ahead).start()

    def line_options(at, way, c, row, slot, rows):
        p = place(way, at)
        options = [(row == at * PAIR + k, rows[k]) for k in range(PAIR)]
        if p == 0:
            return options
        if sends_rows(p - 1, levels):
            return options + [
                (row == place(way, q) * PAIR + k, line_in[way, PAIR * q + k, c])
                for q in range(p) for k in range(PAIR)
            ]
        return options + [(row // PAIR < at if way == 0 else row // PAIR > at, line_in[way, slot, c])]

    def final(at, c):
        rows = level_rows(c)
        options = line_options(at, 0, c, my_row, 0, rows)
        options = options + line_options(at, 1, c, my_row, 0, rows)[PAIR:]
        value = pick(options)
        dest, local = head_of(c)

        @pl.when(dest == sp)
        def _():
            ref_kv[local, sp] = value

        @pl.when(dest != sp)
        def _():
            routed[c] = value
            ref_copy(c, dest, local, sp).start()

    def attend(local, block):
        lanes = pl.ds(pl.multiple_of(local * HEAD_DIM, HEAD_DIM), HEAD_DIM)
        own_keys, ref_keys = n_sp * tokens, n_sp * ref_tokens
        q = q_buf[block, :, lanes]
        k = k_buf[:, :, lanes].reshape(own_keys, HEAD_DIM)
        v = v_buf[:, :, lanes].reshape(own_keys, HEAD_DIM)
        ref_k = ref_kv[local, :, 0].reshape(ref_keys, HEAD_DIM)
        ref_v = ref_kv[local, :, 1].reshape(ref_keys, HEAD_DIM)
        contract = (((1,), (1,)), ((), ()))
        scale = HEAD_DIM ** -0.5
        s_own = lax.dot_general(q, k, contract, preferred_element_type=jnp.float32) * scale
        s_ref = lax.dot_general(q, ref_k, contract, preferred_element_type=jnp.float32) * scale
        col = lax.broadcasted_iota(jnp.int32, s_ref.shape, 1)
        s_ref = jnp.where(col < live, s_ref, -jnp.inf)
        peak = jnp.maximum(
            jnp.max(s_own, axis=1, keepdims=True), jnp.max(s_ref, axis=1, keepdims=True)
        )
        w_own = jnp.exp(s_own - peak)
        w_ref = jnp.exp(s_ref - peak)
        total = jnp.sum(w_own, axis=1, keepdims=True) + jnp.sum(w_ref, axis=1, keepdims=True)
        mixed = jnp.dot(w_own.astype(jnp.bfloat16), v, preferred_element_type=jnp.float32)
        mixed += jnp.dot(w_ref.astype(jnp.bfloat16), ref_v, preferred_element_type=jnp.float32)
        return (mixed / total).astype(jnp.bfloat16)

    last_lag = levels - 2
    units = per_dev * n_sp
    at_once = 2
    first_unit = heads - 1 + last_lag - (per_dev - 1) * n_sp // at_once

    @functools.partial(loop, max(heads + last_lag, first_unit + units // at_once))
    def _(i):
        @pl.when(i + x_ahead < heads)
        def _():
            x_copy(i + x_ahead).start()

        @pl.when(jnp.logical_and(inner, i < heads))
        def _():
            x_copy(i).wait_recv()

        for at in range(levels):
            @pl.when(level == at)
            def _(at=at):
                if at in (0, levels - 1):
                    @pl.when(i + ends_ahead < heads)
                    def _():
                        send_rows(at, i + ends_ahead)

                for way in (0, 1):
                    p = place(way, at)
                    if p == 0:
                        continue
                    c = i - (p - 1)

                    @pl.when(jnp.logical_and(c >= 0, c < heads))
                    def _(c=c, way=way):
                        relay(at, way, c)

                done = i - last_lag

                @pl.when(jnp.logical_and(done >= 0, done < heads))
                def _():
                    final(at, done)

        for n in range(per_step):
            number = i * per_step + n

            @pl.when(number < seq_copies)
            def _(number=number):
                dest = (sp + 1 + number // 3) % n_sp
                for a in range(3):
                    @pl.when(number % 3 == a)
                    def _(a=a):
                        seq_copy(a, dest, sp).start()

        unit = (i - first_unit) * at_once

        @pl.when(jnp.logical_and(unit >= 0, unit < units))
        def _():
            local, turn = unit // n_sp, unit % n_sp

            @pl.when(unit == 0)
            def _():
                for a in range(3):
                    keep_copy(a).wait()

                @functools.partial(loop, n_sp - 1)
                def _(step):
                    src = (sp + 1 + step) % n_sp
                    for a in range(3):
                        seq_copy(a, sp, src).wait_recv()

            @pl.when(turn == 0)
            def _():
                @functools.partial(loop, n_sp - 1)
                def _(step):
                    src = (sp + 1 + step) % n_sp
                    ref_copy(0, sp, local, src).wait_recv()

            lanes = pl.ds(pl.multiple_of(local * HEAD_DIM, HEAD_DIM), HEAD_DIM)
            blocks = [(sp + 1 + turn + n) % n_sp for n in range(at_once)]
            results = [attend(local, block) for block in blocks]
            for block, result in zip(blocks, results):
                o_buf[block, :, lanes] = result
            for block in blocks:
                @pl.when(block == sp)
                def _():
                    o_here(local).start()

                @pl.when(block != sp)
                def _(block=block):
                    o_copy(local, block, sp).start()

    @functools.partial(loop, heads)
    def _(c):
        x_copy(c).wait_send()
        dest, local = head_of(c)

        @pl.when(dest != sp)
        def _():
            ref_copy(c, dest, local, sp).wait_send()

        for at in range(levels):
            @pl.when(level == at)
            def _(at=at):
                for way in (0, 1):
                    p = place(way, at)
                    if p < levels - 1:
                        for slot in range(slots_on(p, levels)):
                            line_copy(way, slot, c, x_buf.at[c], at).wait_send()

    @functools.partial(loop, n_sp - 1)
    def _(step):
        other = (sp + 1 + step) % n_sp
        for a in range(3):
            seq_copy(a, other, sp).wait_send()
        for local in range(per_dev):
            o_copy(local, other, sp).wait_send()
            o_copy(local, sp, other).wait_recv()

    for local in range(per_dev):
        o_here(local).wait()


def shards(n_grp, n_sp, queries, keys, values, ref_cache, ref_ids, ref_owner, ref_lens):
    tokens, width = queries.shape[1:]
    ref_tokens = ref_cache.shape[2]
    heads = width // HEAD_DIM
    per_dev = heads // n_sp
    feat = per_dev * HEAD_DIM
    levels = n_grp // PAIR
    slots = max(slots_on(p, levels) for p in range(levels - 1))
    chunk = (2, ref_tokens, HEAD_DIM)
    bf16 = jnp.bfloat16
    dma = pltpu.SemaphoreType.DMA
    smem = pl.BlockSpec(memory_space=pltpu.SMEM)
    hbm = pl.BlockSpec(memory_space=pl.ANY)
    all_keys = n_sp * (tokens + ref_tokens)
    return pl.pallas_call(
        functools.partial(kernel, n_grp, n_sp),
        out_shape=jax.ShapeDtypeStruct(queries.shape, bf16),
        in_specs=[smem] * 3 + [hbm] * 4,
        out_specs=hbm,
        scratch_shapes=[
            pltpu.VMEM((n_sp, tokens, feat), bf16),
            pltpu.VMEM((n_sp, tokens, feat), bf16),
            pltpu.VMEM((n_sp, tokens, feat), bf16),
            pltpu.VMEM((heads,) + chunk, bf16),
            pltpu.VMEM((heads,) + chunk, bf16),
            pltpu.VMEM((2, slots, heads) + chunk, bf16),
            pltpu.VMEM((2, slots, heads) + chunk, bf16),
            pltpu.VMEM((heads,) + chunk, bf16),
            pltpu.VMEM((per_dev, n_sp) + chunk, bf16),
            pltpu.VMEM((n_sp, tokens, feat), bf16),
            dma((heads,)),
            dma((3,)),
            dma((3, n_sp)),
            dma((3, n_sp)),
            dma((heads,)),
            dma((heads,)),
            dma((2, slots, heads)),
            dma((2, slots, heads)),
            dma((heads,)),
            dma((per_dev, n_sp)),
            dma((per_dev,)),
            dma((per_dev, n_sp)),
            dma((per_dev, n_sp)),
        ],
        compiler_params=pltpu.CompilerParams(
            collective_id=0, has_side_effects=True, vmem_limit_bytes=60 * 1024 * 1024
        ),
        cost_estimate=pl.CostEstimate(
            flops=4 * n_sp * tokens * all_keys * feat,
            bytes_accessed=8 * tokens * width * 2,
            transcendentals=per_dev * n_sp * tokens * all_keys,
        ),
    )(ref_ids, ref_owner, ref_lens, queries, keys, values, ref_cache)


def solution(mesh):
    in_specs = (
        P("grp", "sp", None),
        P("grp", "sp", None),
        P("grp", "sp", None),
        P("grp", None, "sp", None),
        P(),
        P(),
        P(),
    )
    body = functools.partial(shards, mesh.shape["grp"], mesh.shape["sp"])
    return jax.shard_map(
        body, mesh=mesh, in_specs=in_specs, out_specs=P("grp", "sp", None), check_vma=False
    )
```

```python
import functools

import jax
import jax.numpy as jnp
from jax import lax
from jax.experimental import pallas as pl
from jax.experimental.pallas import tpu as pltpu
from jax.sharding import PartitionSpec as P

HEAD_DIM = 128
PAIR = 2
MESH = pl.DeviceIdType.MESH


def slots_on(p, levels):
    return min(PAIR * (p + 1), levels - 1 - p)


def sends_rows(p, levels):
    return PAIR * (p + 1) <= levels - 1 - p


def pick(options):
    value = options[-1][1]
    for cond, other in reversed(options[:-1]):
        value = lax.select(cond, other, value)
    return value


def kernel(
    n_grp, n_sp,
    ids_ref, owner_ref, lens_ref, q_hbm, k_hbm, v_hbm, ref_hbm, out_hbm,
    q_buf, k_buf, v_buf, own_buf, x_buf, line_in, line_out, routed, ref_kv, o_buf,
    own_sem, keep_sem, seq_send, seq_recv, x_send, x_recv, line_send, line_recv,
    ref_send, ref_recv, o_keep, o_send, o_recv,
):
    levels = n_grp // PAIR
    heads = ref_hbm.shape[-1] // HEAD_DIM
    per_dev = heads // n_sp
    feat = per_dev * HEAD_DIM
    tokens = q_hbm.shape[1]
    ref_tokens = ref_hbm.shape[2]
    grp = lax.axis_index("grp")
    sp = lax.axis_index("sp")
    level = grp // PAIR
    side = grp % PAIR
    mate = level * PAIR + (1 - side)

    def at_level(other):
        return (other * PAIR + side, sp)

    barrier = pltpu.get_barrier_semaphore()

    def greet(device):
        pl.semaphore_signal(barrier, inc=1, device_id=device, device_id_type=MESH)

    greet((mate, sp))
    for step in range(1, n_sp):
        greet((grp, (sp + step) % n_sp))

    @pl.when(level > 0)
    def _():
        greet(at_level(level - 1))

    @pl.when(level < levels - 1)
    def _():
        greet(at_level(level + 1))

    inner = jnp.logical_and(level > 0, level < levels - 1)
    pl.semaphore_wait(barrier, n_sp + 1 + inner.astype(jnp.int32))

    def head_of(c):
        return (c + sp) % n_sp, c // n_sp

    def lanes_of(c):
        dest, local = head_of(c)
        return pl.ds(pl.multiple_of((dest * per_dev + local) * HEAD_DIM, HEAD_DIM), HEAD_DIM)

    def own_copy(c):
        return pltpu.make_async_copy(
            ref_hbm.at[0, :, :, lanes_of(c)], own_buf.at[c], own_sem.at[c]
        )

    def x_copy(c):
        return pltpu.make_async_remote_copy(
            src_ref=ref_hbm.at[0, :, :, lanes_of(c)], dst_ref=x_buf.at[c],
            send_sem=x_send.at[c], recv_sem=x_recv.at[c],
            device_id=(mate, sp), device_id_type=MESH,
        )

    def line_copy(way, slot, c, src, other):
        return pltpu.make_async_remote_copy(
            src_ref=src, dst_ref=line_in.at[way, slot, c],
            send_sem=line_send.at[way, slot, c], recv_sem=line_recv.at[way, slot, c],
            device_id=at_level(other), device_id_type=MESH,
        )

    def ref_copy(c, dest, local, src):
        return pltpu.make_async_remote_copy(
            src_ref=routed.at[c], dst_ref=ref_kv.at[local, src],
            send_sem=ref_send.at[c], recv_sem=ref_recv.at[local, src],
            device_id=(grp, dest), device_id_type=MESH,
        )

    seq_pairs = ((q_hbm, q_buf), (k_hbm, k_buf), (v_hbm, v_buf))

    def seq_lanes(dest):
        return pl.ds(pl.multiple_of(dest * feat, HEAD_DIM), feat)

    def seq_copy(a, dest, src):
        hbm, buf = seq_pairs[a]
        return pltpu.make_async_remote_copy(
            src_ref=hbm.at[0, :, seq_lanes(dest)], dst_ref=buf.at[src],
            send_sem=seq_send.at[a, dest], recv_sem=seq_recv.at[a, src],
            device_id=(grp, dest), device_id_type=MESH,
        )

    def keep_copy(a):
        hbm, buf = seq_pairs[a]
        return pltpu.make_async_copy(
            hbm.at[0, :, seq_lanes(sp)], buf.at[sp], keep_sem.at[a]
        )

    def o_copy(local, dest, src):
        lanes = pl.ds(pl.multiple_of(local * HEAD_DIM, HEAD_DIM), HEAD_DIM)
        out_lanes = pl.ds(pl.multiple_of(src * feat + local * HEAD_DIM, HEAD_DIM), HEAD_DIM)
        return pltpu.make_async_remote_copy(
            src_ref=o_buf.at[dest, :, lanes], dst_ref=out_hbm.at[0, :, out_lanes],
            send_sem=o_send.at[local, dest], recv_sem=o_recv.at[local, src],
            device_id=(grp, dest), device_id_type=MESH,
        )

    def o_here(local):
        lanes = pl.ds(pl.multiple_of(local * HEAD_DIM, HEAD_DIM), HEAD_DIM)
        out_lanes = pl.ds(pl.multiple_of(sp * feat + local * HEAD_DIM, HEAD_DIM), HEAD_DIM)
        return pltpu.make_async_copy(
            o_buf.at[sp, :, lanes], out_hbm.at[0, :, out_lanes], o_keep.at[local]
        )

    def loop(count, body):
        def step(i, carry):
            body(i)
            return carry
        lax.fori_loop(0, count, step, 0)

    x_ahead, ends_ahead = 8, 6
    seq_copies = 3 * (n_sp - 1)
    per_step = -(-seq_copies // 9)

    @functools.partial(loop, x_ahead)
    def _(c):
        x_copy(c).start()

    @functools.partial(loop, heads)
    def _(c):
        own_copy(c).start()

    for a in range(3):
        keep_copy(a).start()

    @functools.partial(loop, heads)
    def _(c):
        own_copy(c).wait()

    wanted = [owner_ref[ids_ref[lev * PAIR + side]] for lev in range(levels)]
    here = ids_ref[grp]
    my_row = owner_ref[here]
    live = lens_ref[here]

    def level_rows(c):
        own, other = own_buf[c], x_buf[c]
        return [lax.select(side == k, own, other) for k in range(PAIR)]

    def send_rows(at, c):
        way, ahead = (0, at + 1) if at == 0 else (1, at - 1)
        line_copy(way, side, c, own_buf.at[c], ahead).start()
        x_copy(c).wait_recv()
        line_copy(way, 1 - side, c, x_buf.at[c], ahead).start()

    for at in (0, levels - 1):
        @pl.when(level == at)
        def _(at=at):
            @functools.partial(loop, ends_ahead)
            def _(c):
                send_rows(at, c)

    def place(way, lev):
        return lev if way == 0 else levels - 1 - lev

    def relay(at, way, c):
        p = place(way, at)
        ahead = at + 1 if way == 0 else at - 1
        for slot in range(slots_on(p - 1, levels)):
            line_copy(way, slot, c, x_buf.at[c], at).wait_recv()
        if p == levels - 1:
            return
        count = slots_on(p, levels)
        if sends_rows(p, levels):
            for slot in range(PAIR * p):
                line_copy(way, slot, c, line_in.at[way, slot, c], ahead).start()
            line_copy(way, PAIR * p + side, c, own_buf.at[c], ahead).start()
            line_copy(way, PAIR * p + 1 - side, c, x_buf.at[c], ahead).start()
            return
        rows = level_rows(c)
        for slot in range(count):
            row = wanted[place(way, p + 1 + slot)]
            value = pick(line_options(at, way, c, row, slot + 1, rows))
            line_out[way, slot, c] = value
            line_copy(way, slot, c, line_out.at[way, slot, c], ahead).start()

    def line_options(at, way, c, row, slot, rows):
        p = place(way, at)
        options = [(row == at * PAIR + k, rows[k]) for k in range(PAIR)]
        if p == 0:
            return options
        if sends_rows(p - 1, levels):
            return options + [
                (row == place(way, q) * PAIR + k, line_in[way, PAIR * q + k, c])
                for q in range(p) for k in range(PAIR)
            ]
        return options + [(row // PAIR < at if way == 0 else row // PAIR > at, line_in[way, slot, c])]

    def final(at, c):
        rows = level_rows(c)
        options = line_options(at, 0, c, my_row, 0, rows)
        options = options + line_options(at, 1, c, my_row, 0, rows)[PAIR:]
        value = pick(options)
        dest, local = head_of(c)

        @pl.when(dest == sp)
        def _():
            ref_kv[local, sp] = value

        @pl.when(dest != sp)
        def _():
            routed[c] = value
            ref_copy(c, dest, local, sp).start()

    def attend(local, block):
        lanes = pl.ds(pl.multiple_of(local * HEAD_DIM, HEAD_DIM), HEAD_DIM)
        own_keys, ref_keys = n_sp * tokens, n_sp * ref_tokens
        q = q_buf[block, :, lanes]
        k = k_buf[:, :, lanes].reshape(own_keys, HEAD_DIM)
        v = v_buf[:, :, lanes].reshape(own_keys, HEAD_DIM)
        ref_k = ref_kv[local, :, 0].reshape(ref_keys, HEAD_DIM)
        ref_v = ref_kv[local, :, 1].reshape(ref_keys, HEAD_DIM)
        contract = (((1,), (1,)), ((), ()))
        scale = HEAD_DIM ** -0.5
        s_own = lax.dot_general(q, k, contract, preferred_element_type=jnp.float32) * scale
        s_ref = lax.dot_general(q, ref_k, contract, preferred_element_type=jnp.float32) * scale
        col = lax.broadcasted_iota(jnp.int32, s_ref.shape, 1)
        s_ref = jnp.where(col < live, s_ref, -jnp.inf)
        peak = jnp.maximum(
            jnp.max(s_own, axis=1, keepdims=True), jnp.max(s_ref, axis=1, keepdims=True)
        )
        w_own = jnp.exp(s_own - peak)
        w_ref = jnp.exp(s_ref - peak)
        total = jnp.sum(w_own, axis=1, keepdims=True) + jnp.sum(w_ref, axis=1, keepdims=True)
        mixed = jnp.dot(w_own.astype(jnp.bfloat16), v, preferred_element_type=jnp.float32)
        mixed += jnp.dot(w_ref.astype(jnp.bfloat16), ref_v, preferred_element_type=jnp.float32)
        return (mixed / total).astype(jnp.bfloat16)

    last_lag = levels - 1
    units = per_dev * n_sp
    at_once = 2
    first_unit = heads - 1 + last_lag - (per_dev - 1) * n_sp // at_once

    @functools.partial(loop, max(heads + last_lag, first_unit + units // at_once))
    def _(i):
        @pl.when(i + x_ahead < heads)
        def _():
            x_copy(i + x_ahead).start()

        @pl.when(jnp.logical_and(inner, i < heads))
        def _():
            x_copy(i).wait_recv()

        for at in range(levels):
            @pl.when(level == at)
            def _(at=at):
                if at in (0, levels - 1):
                    @pl.when(i + ends_ahead < heads)
                    def _():
                        send_rows(at, i + ends_ahead)

                for p, way in sorted((place(way, at), way) for way in (0, 1)):
                    if p == 0:
                        continue
                    c = i - (0 if p == 1 else p)

                    @pl.when(jnp.logical_and(c >= 0, c < heads))
                    def _(c=c, way=way):
                        relay(at, way, c)

                done = i - last_lag

                @pl.when(jnp.logical_and(done >= 0, done < heads))
                def _():
                    final(at, done)

        for n in range(per_step):
            number = i * per_step + n

            @pl.when(number < seq_copies)
            def _(number=number):
                dest = (sp + 1 + number // 3) % n_sp
                for a in range(3):
                    @pl.when(number % 3 == a)
                    def _(a=a):
                        seq_copy(a, dest, sp).start()

        unit = (i - first_unit) * at_once

        @pl.when(jnp.logical_and(unit >= 0, unit < units))
        def _():
            local, turn = unit // n_sp, unit % n_sp

            @pl.when(unit == 0)
            def _():
                for a in range(3):
                    keep_copy(a).wait()

                @functools.partial(loop, n_sp - 1)
                def _(step):
                    src = (sp + 1 + step) % n_sp
                    for a in range(3):
                        seq_copy(a, sp, src).wait_recv()

            @pl.when(turn == 0)
            def _():
                @functools.partial(loop, n_sp - 1)
                def _(step):
                    src = (sp + 1 + step) % n_sp
                    ref_copy(0, sp, local, src).wait_recv()

            lanes = pl.ds(pl.multiple_of(local * HEAD_DIM, HEAD_DIM), HEAD_DIM)
            blocks = [(sp + 1 + turn + n) % n_sp for n in range(at_once)]
            results = [attend(local, block) for block in blocks]
            for block, result in zip(blocks, results):
                o_buf[block, :, lanes] = result
            for block in blocks:
                @pl.when(block == sp)
                def _():
                    o_here(local).start()

                @pl.when(block != sp)
                def _(block=block):
                    o_copy(local, block, sp).start()

    @functools.partial(loop, heads)
    def _(c):
        x_copy(c).wait_send()
        dest, local = head_of(c)

        @pl.when(dest != sp)
        def _():
            ref_copy(c, dest, local, sp).wait_send()

        for at in range(levels):
            @pl.when(level == at)
            def _(at=at):
                for way in (0, 1):
                    p = place(way, at)
                    if p < levels - 1:
                        for slot in range(slots_on(p, levels)):
                            line_copy(way, slot, c, x_buf.at[c], at).wait_send()

    @functools.partial(loop, n_sp - 1)
    def _(step):
        other = (sp + 1 + step) % n_sp
        for a in range(3):
            seq_copy(a, other, sp).wait_send()
        for local in range(per_dev):
            o_copy(local, other, sp).wait_send()
            o_copy(local, sp, other).wait_recv()

    for local in range(per_dev):
        o_here(local).wait()


def shards(n_grp, n_sp, queries, keys, values, ref_cache, ref_ids, ref_owner, ref_lens):
    tokens, width = queries.shape[1:]
    ref_tokens = ref_cache.shape[2]
    heads = width // HEAD_DIM
    per_dev = heads // n_sp
    feat = per_dev * HEAD_DIM
    levels = n_grp // PAIR
    slots = max(slots_on(p, levels) for p in range(levels - 1))
    chunk = (2, ref_tokens, HEAD_DIM)
    bf16 = jnp.bfloat16
    dma = pltpu.SemaphoreType.DMA
    smem = pl.BlockSpec(memory_space=pltpu.SMEM)
    hbm = pl.BlockSpec(memory_space=pl.ANY)
    all_keys = n_sp * (tokens + ref_tokens)
    return pl.pallas_call(
        functools.partial(kernel, n_grp, n_sp),
        out_shape=jax.ShapeDtypeStruct(queries.shape, bf16),
        in_specs=[smem] * 3 + [hbm] * 4,
        out_specs=hbm,
        scratch_shapes=[
            pltpu.VMEM((n_sp, tokens, feat), bf16),
            pltpu.VMEM((n_sp, tokens, feat), bf16),
            pltpu.VMEM((n_sp, tokens, feat), bf16),
            pltpu.VMEM((heads,) + chunk, bf16),
            pltpu.VMEM((heads,) + chunk, bf16),
            pltpu.VMEM((2, slots, heads) + chunk, bf16),
            pltpu.VMEM((2, slots, heads) + chunk, bf16),
            pltpu.VMEM((heads,) + chunk, bf16),
            pltpu.VMEM((per_dev, n_sp) + chunk, bf16),
            pltpu.VMEM((n_sp, tokens, feat), bf16),
            dma((heads,)),
            dma((3,)),
            dma((3, n_sp)),
            dma((3, n_sp)),
            dma((heads,)),
            dma((heads,)),
            dma((2, slots, heads)),
            dma((2, slots, heads)),
            dma((heads,)),
            dma((per_dev, n_sp)),
            dma((per_dev,)),
            dma((per_dev, n_sp)),
            dma((per_dev, n_sp)),
        ],
        compiler_params=pltpu.CompilerParams(
            collective_id=0, has_side_effects=True, vmem_limit_bytes=60 * 1024 * 1024
        ),
        cost_estimate=pl.CostEstimate(
            flops=4 * n_sp * tokens * all_keys * feat,
            bytes_accessed=8 * tokens * width * 2,
            transcendentals=per_dev * n_sp * tokens * all_keys,
        ),
    )(ref_ids, ref_owner, ref_lens, queries, keys, values, ref_cache)


def solution(mesh):
    in_specs = (
        P("grp", "sp", None),
        P("grp", "sp", None),
        P("grp", "sp", None),
        P("grp", None, "sp", None),
        P(),
        P(),
        P(),
    )
    body = functools.partial(shards, mesh.shape["grp"], mesh.shape["sp"])
    return jax.shard_map(
        body, mesh=mesh, in_specs=in_specs, out_specs=P("grp", "sp", None), check_vma=False
    )
```

```python
import functools

import jax
import jax.numpy as jnp
from jax import lax
from jax.experimental import pallas as pl
from jax.experimental.pallas import tpu as pltpu
from jax.sharding import PartitionSpec as P

HEAD_DIM = 128
PAIR = 2
MESH = pl.DeviceIdType.MESH


def slots_on(p, levels):
    return min(PAIR * (p + 1), levels - 1 - p)


def sends_rows(p, levels):
    return PAIR * (p + 1) <= levels - 1 - p


def pick(options):
    value = options[-1][1]
    for cond, other in reversed(options[:-1]):
        value = lax.select(cond, other, value)
    return value


def kernel(
    n_grp, n_sp,
    ids_ref, owner_ref, lens_ref, q_hbm, k_hbm, v_hbm, ref_hbm, out_hbm,
    q_buf, k_buf, v_buf, own_buf, x_buf, line_in, line_out, routed, ref_kv, o_buf,
    own_sem, keep_sem, seq_send, seq_recv, x_send, x_recv, line_send, line_recv,
    ref_send, ref_recv, o_keep, o_send, o_recv,
):
    levels = n_grp // PAIR
    heads = ref_hbm.shape[-1] // HEAD_DIM
    per_dev = heads // n_sp
    feat = per_dev * HEAD_DIM
    tokens = q_hbm.shape[1]
    ref_tokens = ref_hbm.shape[2]
    grp = lax.axis_index("grp")
    sp = lax.axis_index("sp")
    level = grp // PAIR
    side = grp % PAIR
    mate = level * PAIR + (1 - side)

    def at_level(other):
        return (other * PAIR + side, sp)

    barrier = pltpu.get_barrier_semaphore()

    def greet(device):
        pl.semaphore_signal(barrier, inc=1, device_id=device, device_id_type=MESH)

    greet((mate, sp))
    for step in range(1, n_sp):
        greet((grp, (sp + step) % n_sp))

    @pl.when(level > 0)
    def _():
        greet(at_level(level - 1))

    @pl.when(level < levels - 1)
    def _():
        greet(at_level(level + 1))

    inner = jnp.logical_and(level > 0, level < levels - 1)
    pl.semaphore_wait(barrier, n_sp + 1 + inner.astype(jnp.int32))

    def head_of(c):
        return (c + sp) % n_sp, c // n_sp

    def lanes_of(c):
        dest, local = head_of(c)
        return pl.ds(pl.multiple_of((dest * per_dev + local) * HEAD_DIM, HEAD_DIM), HEAD_DIM)

    def own_copy(c):
        return pltpu.make_async_copy(
            ref_hbm.at[0, :, :, lanes_of(c)], own_buf.at[c], own_sem.at[c]
        )

    def x_copy(c):
        return pltpu.make_async_remote_copy(
            src_ref=ref_hbm.at[0, :, :, lanes_of(c)], dst_ref=x_buf.at[c],
            send_sem=x_send.at[c], recv_sem=x_recv.at[c],
            device_id=(mate, sp), device_id_type=MESH,
        )

    def line_copy(way, slot, c, src, other):
        return pltpu.make_async_remote_copy(
            src_ref=src, dst_ref=line_in.at[way, slot, c],
            send_sem=line_send.at[way, slot, c], recv_sem=line_recv.at[way, slot, c],
            device_id=at_level(other), device_id_type=MESH,
        )

    def ref_copy(c, dest, local, src):
        return pltpu.make_async_remote_copy(
            src_ref=routed.at[c], dst_ref=ref_kv.at[local, src],
            send_sem=ref_send.at[c], recv_sem=ref_recv.at[local, src],
            device_id=(grp, dest), device_id_type=MESH,
        )

    seq_pairs = ((q_hbm, q_buf), (k_hbm, k_buf), (v_hbm, v_buf))

    def seq_lanes(dest):
        return pl.ds(pl.multiple_of(dest * feat, HEAD_DIM), feat)

    def seq_copy(a, dest, src):
        hbm, buf = seq_pairs[a]
        return pltpu.make_async_remote_copy(
            src_ref=hbm.at[0, :, seq_lanes(dest)], dst_ref=buf.at[src],
            send_sem=seq_send.at[a, dest], recv_sem=seq_recv.at[a, src],
            device_id=(grp, dest), device_id_type=MESH,
        )

    def keep_copy(a):
        hbm, buf = seq_pairs[a]
        return pltpu.make_async_copy(
            hbm.at[0, :, seq_lanes(sp)], buf.at[sp], keep_sem.at[a]
        )

    def o_copy(local, dest, src):
        lanes = pl.ds(pl.multiple_of(local * HEAD_DIM, HEAD_DIM), HEAD_DIM)
        out_lanes = pl.ds(pl.multiple_of(src * feat + local * HEAD_DIM, HEAD_DIM), HEAD_DIM)
        return pltpu.make_async_remote_copy(
            src_ref=o_buf.at[dest, :, lanes], dst_ref=out_hbm.at[0, :, out_lanes],
            send_sem=o_send.at[local, dest], recv_sem=o_recv.at[local, src],
            device_id=(grp, dest), device_id_type=MESH,
        )

    def o_here(local):
        lanes = pl.ds(pl.multiple_of(local * HEAD_DIM, HEAD_DIM), HEAD_DIM)
        out_lanes = pl.ds(pl.multiple_of(sp * feat + local * HEAD_DIM, HEAD_DIM), HEAD_DIM)
        return pltpu.make_async_copy(
            o_buf.at[sp, :, lanes], out_hbm.at[0, :, out_lanes], o_keep.at[local]
        )

    def loop(count, body):
        def step(i, carry):
            body(i)
            return carry
        lax.fori_loop(0, count, step, 0)

    x_ahead, ends_ahead = 10, 8
    seq_copies = 3 * (n_sp - 1)
    per_step = -(-seq_copies // 9)

    @functools.partial(loop, x_ahead)
    def _(c):
        x_copy(c).start()

    wanted = [owner_ref[ids_ref[lev * PAIR + side]] for lev in range(levels)]
    here = ids_ref[grp]
    my_row = owner_ref[here]
    live = lens_ref[here]

    def level_rows(c):
        own, other = own_buf[c], x_buf[c]
        return [lax.select(side == k, own, other) for k in range(PAIR)]

    def send_own(at, c):
        way, ahead = (0, at + 1) if at == 0 else (1, at - 1)
        own = ref_hbm.at[0, :, :, lanes_of(c)]
        line_copy(way, side, c, own, ahead).start()

    def send_other(at, c):
        way, ahead = (0, at + 1) if at == 0 else (1, at - 1)
        x_copy(c).wait_recv()
        line_copy(way, 1 - side, c, x_buf.at[c], ahead).start()

    for at in (0, levels - 1):
        @pl.when(level == at)
        def _(at=at):
            @functools.partial(loop, ends_ahead)
            def _(c):
                send_own(at, c)

    @functools.partial(loop, heads)
    def _(c):
        own_copy(c).start()

    for a in range(3):
        keep_copy(a).start()

    for at in (0, levels - 1):
        @pl.when(level == at)
        def _(at=at):
            @functools.partial(loop, ends_ahead)
            def _(c):
                send_other(at, c)

    def place(way, lev):
        return lev if way == 0 else levels - 1 - lev

    def relay(at, way, c):
        p = place(way, at)
        ahead = at + 1 if way == 0 else at - 1
        for slot in range(slots_on(p - 1, levels)):
            line_copy(way, slot, c, x_buf.at[c], at).wait_recv()
        if p == levels - 1:
            return
        count = slots_on(p, levels)
        if sends_rows(p, levels):
            for slot in range(PAIR * p):
                line_copy(way, slot, c, line_in.at[way, slot, c], ahead).start()
            line_copy(way, PAIR * p + side, c, own_buf.at[c], ahead).start()
            line_copy(way, PAIR * p + 1 - side, c, x_buf.at[c], ahead).start()
            return
        rows = level_rows(c)
        for slot in range(count):
            row = wanted[place(way, p + 1 + slot)]
            value = pick(line_options(at, way, c, row, slot + 1, rows))
            line_out[way, slot, c] = value
            line_copy(way, slot, c, line_out.at[way, slot, c], ahead).start()

    def line_options(at, way, c, row, slot, rows):
        p = place(way, at)
        options = [(row == at * PAIR + k, rows[k]) for k in range(PAIR)]
        if p == 0:
            return options
        if sends_rows(p - 1, levels):
            return options + [
                (row == place(way, q) * PAIR + k, line_in[way, PAIR * q + k, c])
                for q in range(p) for k in range(PAIR)
            ]
        return options + [(row // PAIR < at if way == 0 else row // PAIR > at, line_in[way, slot, c])]

    def final(at, c):
        rows = level_rows(c)
        options = line_options(at, 0, c, my_row, 0, rows)
        options = options + line_options(at, 1, c, my_row, 0, rows)[PAIR:]
        value = pick(options)
        dest, local = head_of(c)

        @pl.when(dest == sp)
        def _():
            ref_kv[local, sp] = value

        @pl.when(dest != sp)
        def _():
            routed[c] = value
            ref_copy(c, dest, local, sp).start()

    def attend(local, block):
        lanes = pl.ds(pl.multiple_of(local * HEAD_DIM, HEAD_DIM), HEAD_DIM)
        own_keys, ref_keys = n_sp * tokens, n_sp * ref_tokens
        q = q_buf[block, :, lanes]
        k = k_buf[:, :, lanes].reshape(own_keys, HEAD_DIM)
        v = v_buf[:, :, lanes].reshape(own_keys, HEAD_DIM)
        ref_k = ref_kv[local, :, 0].reshape(ref_keys, HEAD_DIM)
        ref_v = ref_kv[local, :, 1].reshape(ref_keys, HEAD_DIM)
        contract = (((1,), (1,)), ((), ()))
        scale = HEAD_DIM ** -0.5
        s_own = lax.dot_general(q, k, contract, preferred_element_type=jnp.float32) * scale
        s_ref = lax.dot_general(q, ref_k, contract, preferred_element_type=jnp.float32) * scale
        col = lax.broadcasted_iota(jnp.int32, s_ref.shape, 1)
        s_ref = jnp.where(col < live, s_ref, -jnp.inf)
        peak = jnp.maximum(
            jnp.max(s_own, axis=1, keepdims=True), jnp.max(s_ref, axis=1, keepdims=True)
        )
        w_own = jnp.exp(s_own - peak)
        w_ref = jnp.exp(s_ref - peak)
        total = jnp.sum(w_own, axis=1, keepdims=True) + jnp.sum(w_ref, axis=1, keepdims=True)
        mixed = jnp.dot(w_own.astype(jnp.bfloat16), v, preferred_element_type=jnp.float32)
        mixed += jnp.dot(w_ref.astype(jnp.bfloat16), ref_v, preferred_element_type=jnp.float32)
        return (mixed / total).astype(jnp.bfloat16)

    last_lag = levels
    units = per_dev * n_sp
    at_once = 2
    per_head = n_sp // at_once
    last_start = heads - 1 + last_lag
    first_unit = max(
        [3 * heads // 4]
        + [(n + 1) * n_sp - 1 + last_lag - n * per_head for n in range(per_dev - 1)]
    )

    @functools.partial(loop, last_start + per_head)
    def _(i):
        @pl.when(i + x_ahead < heads)
        def _():
            x_copy(i + x_ahead).start()

        @pl.when(jnp.logical_and(inner, i < heads))
        def _():
            x_copy(i).wait_recv()

        @pl.when(i < heads)
        def _():
            own_copy(i).wait()

        for at in range(levels):
            @pl.when(level == at)
            def _(at=at):
                if at in (0, levels - 1):
                    @pl.when(i + ends_ahead < heads)
                    def _():
                        send_own(at, i + ends_ahead)
                        send_other(at, i + ends_ahead)

                for p, way in sorted((place(way, at), way) for way in (0, 1)):
                    if p == 0:
                        continue
                    c = i - (0 if p == 1 else p + 1)

                    @pl.when(jnp.logical_and(c >= 0, c < heads))
                    def _(c=c, way=way):
                        relay(at, way, c)

                done = i - last_lag

                @pl.when(jnp.logical_and(done >= 0, done < heads))
                def _():
                    final(at, done)

        for n in range(per_step):
            number = i * per_step + n

            @pl.when(number < seq_copies)
            def _(number=number):
                dest = (sp + 1 + number // 3) % n_sp
                for a in range(3):
                    @pl.when(number % 3 == a)
                    def _(a=a):
                        seq_copy(a, dest, sp).start()

        early = (i - first_unit) * at_once
        late = (i - last_start) * at_once + units - n_sp
        unit = jnp.where(i >= last_start, late, early)
        due = jnp.logical_or(
            jnp.logical_and(early >= 0, early < units - n_sp), i >= last_start
        )

        @pl.when(due)
        def _():
            local, turn = unit // n_sp, unit % n_sp

            @pl.when(unit == 0)
            def _():
                for a in range(3):
                    keep_copy(a).wait()

                @functools.partial(loop, n_sp - 1)
                def _(step):
                    src = (sp + 1 + step) % n_sp
                    for a in range(3):
                        seq_copy(a, sp, src).wait_recv()

            @pl.when(turn == 0)
            def _():
                @functools.partial(loop, n_sp - 1)
                def _(step):
                    src = (sp + 1 + step) % n_sp
                    ref_copy(0, sp, local, src).wait_recv()

            lanes = pl.ds(pl.multiple_of(local * HEAD_DIM, HEAD_DIM), HEAD_DIM)
            blocks = [(sp + 1 + turn + n) % n_sp for n in range(at_once)]
            results = [attend(local, block) for block in blocks]
            for block, result in zip(blocks, results):
                o_buf[block, :, lanes] = result
            for block in blocks:
                @pl.when(block == sp)
                def _():
                    o_here(local).start()

                @pl.when(block != sp)
                def _(block=block):
                    o_copy(local, block, sp).start()

    @functools.partial(loop, heads)
    def _(c):
        x_copy(c).wait_send()
        dest, local = head_of(c)

        @pl.when(dest != sp)
        def _():
            ref_copy(c, dest, local, sp).wait_send()

        for at in range(levels):
            @pl.when(level == at)
            def _(at=at):
                for way in (0, 1):
                    p = place(way, at)
                    if p < levels - 1:
                        for slot in range(slots_on(p, levels)):
                            line_copy(way, slot, c, x_buf.at[c], at).wait_send()

    @functools.partial(loop, n_sp - 1)
    def _(step):
        other = (sp + 1 + step) % n_sp
        for a in range(3):
            seq_copy(a, other, sp).wait_send()
        for local in range(per_dev):
            o_copy(local, other, sp).wait_send()
            o_copy(local, sp, other).wait_recv()

    for local in range(per_dev):
        o_here(local).wait()


def shards(n_grp, n_sp, queries, keys, values, ref_cache, ref_ids, ref_owner, ref_lens):
    tokens, width = queries.shape[1:]
    ref_tokens = ref_cache.shape[2]
    heads = width // HEAD_DIM
    per_dev = heads // n_sp
    feat = per_dev * HEAD_DIM
    levels = n_grp // PAIR
    slots = max(slots_on(p, levels) for p in range(levels - 1))
    chunk = (2, ref_tokens, HEAD_DIM)
    bf16 = jnp.bfloat16
    dma = pltpu.SemaphoreType.DMA
    smem = pl.BlockSpec(memory_space=pltpu.SMEM)
    hbm = pl.BlockSpec(memory_space=pl.ANY)
    all_keys = n_sp * (tokens + ref_tokens)
    return pl.pallas_call(
        functools.partial(kernel, n_grp, n_sp),
        out_shape=jax.ShapeDtypeStruct(queries.shape, bf16),
        in_specs=[smem] * 3 + [hbm] * 4,
        out_specs=hbm,
        scratch_shapes=[
            pltpu.VMEM((n_sp, tokens, feat), bf16),
            pltpu.VMEM((n_sp, tokens, feat), bf16),
            pltpu.VMEM((n_sp, tokens, feat), bf16),
            pltpu.VMEM((heads,) + chunk, bf16),
            pltpu.VMEM((heads,) + chunk, bf16),
            pltpu.VMEM((2, slots, heads) + chunk, bf16),
            pltpu.VMEM((2, slots, heads) + chunk, bf16),
            pltpu.VMEM((heads,) + chunk, bf16),
            pltpu.VMEM((per_dev, n_sp) + chunk, bf16),
            pltpu.VMEM((n_sp, tokens, feat), bf16),
            dma((heads,)),
            dma((3,)),
            dma((3, n_sp)),
            dma((3, n_sp)),
            dma((heads,)),
            dma((heads,)),
            dma((2, slots, heads)),
            dma((2, slots, heads)),
            dma((heads,)),
            dma((per_dev, n_sp)),
            dma((per_dev,)),
            dma((per_dev, n_sp)),
            dma((per_dev, n_sp)),
        ],
        compiler_params=pltpu.CompilerParams(
            collective_id=0, has_side_effects=True, vmem_limit_bytes=60 * 1024 * 1024
        ),
        cost_estimate=pl.CostEstimate(
            flops=4 * n_sp * tokens * all_keys * feat,
            bytes_accessed=8 * tokens * width * 2,
            transcendentals=per_dev * n_sp * tokens * all_keys,
        ),
    )(ref_ids, ref_owner, ref_lens, queries, keys, values, ref_cache)


def solution(mesh):
    in_specs = (
        P("grp", "sp", None),
        P("grp", "sp", None),
        P("grp", "sp", None),
        P("grp", None, "sp", None),
        P(),
        P(),
        P(),
    )
    body = functools.partial(shards, mesh.shape["grp"], mesh.shape["sp"])
    return jax.shard_map(
        body, mesh=mesh, in_specs=in_specs, out_specs=P("grp", "sp", None), check_vma=False
    )
```

```python
import functools

import jax
import jax.numpy as jnp
from jax import lax
from jax.experimental import pallas as pl
from jax.experimental.pallas import tpu as pltpu
from jax.sharding import PartitionSpec as P

HEAD_DIM = 128
PAIR = 2
MESH = pl.DeviceIdType.MESH


def slots_on(p, levels):
    return min(PAIR * (p + 1), levels - 1 - p)


def sends_rows(p, levels):
    return PAIR * (p + 1) <= levels - 1 - p


def pick(options):
    value = options[-1][1]
    for cond, other in reversed(options[:-1]):
        value = lax.select(cond, other, value)
    return value


def kernel(
    n_grp, n_sp,
    ids_ref, owner_ref, lens_ref, q_hbm, k_hbm, v_hbm, ref_hbm, out_hbm,
    q_buf, k_buf, v_buf, own_buf, x_buf, line_in, line_out, routed, ref_kv, o_buf,
    own_sem, keep_sem, seq_send, seq_recv, x_send, x_recv, line_send, line_recv,
    ref_send, ref_recv, o_keep, o_send, o_recv,
):
    levels = n_grp // PAIR
    heads = ref_hbm.shape[-1] // HEAD_DIM
    per_dev = heads // n_sp
    feat = per_dev * HEAD_DIM
    tokens = q_hbm.shape[1]
    ref_tokens = ref_hbm.shape[2]
    grp = lax.axis_index("grp")
    sp = lax.axis_index("sp")
    level = grp // PAIR
    side = grp % PAIR
    mate = level * PAIR + (1 - side)

    def at_level(other):
        return (other * PAIR + side, sp)

    barrier = pltpu.get_barrier_semaphore()

    def greet(device):
        pl.semaphore_signal(barrier, inc=1, device_id=device, device_id_type=MESH)

    greet((mate, sp))
    for step in range(1, n_sp):
        greet((grp, (sp + step) % n_sp))

    @pl.when(level > 0)
    def _():
        greet(at_level(level - 1))

    @pl.when(level < levels - 1)
    def _():
        greet(at_level(level + 1))

    inner = jnp.logical_and(level > 0, level < levels - 1)
    pl.semaphore_wait(barrier, n_sp + 1 + inner.astype(jnp.int32))

    def head_of(c):
        return (c + sp) % n_sp, c // n_sp

    def lanes_of(c):
        dest, local = head_of(c)
        return pl.ds(pl.multiple_of((dest * per_dev + local) * HEAD_DIM, HEAD_DIM), HEAD_DIM)

    def own_copy(c):
        return pltpu.make_async_copy(
            ref_hbm.at[0, :, :, lanes_of(c)], own_buf.at[c], own_sem.at[c]
        )

    def x_copy(c):
        return pltpu.make_async_remote_copy(
            src_ref=ref_hbm.at[0, :, :, lanes_of(c)], dst_ref=x_buf.at[c],
            send_sem=x_send.at[c], recv_sem=x_recv.at[c],
            device_id=(mate, sp), device_id_type=MESH,
        )

    def line_copy(way, slot, c, src, other):
        return pltpu.make_async_remote_copy(
            src_ref=src, dst_ref=line_in.at[way, slot, c],
            send_sem=line_send.at[way, slot, c], recv_sem=line_recv.at[way, slot, c],
            device_id=at_level(other), device_id_type=MESH,
        )

    def ref_copy(c, dest, local, src):
        return pltpu.make_async_remote_copy(
            src_ref=routed.at[c], dst_ref=ref_kv.at[local, src],
            send_sem=ref_send.at[c], recv_sem=ref_recv.at[local, src],
            device_id=(grp, dest), device_id_type=MESH,
        )

    seq_pairs = ((q_hbm, q_buf), (k_hbm, k_buf), (v_hbm, v_buf))

    def seq_lanes(dest):
        return pl.ds(pl.multiple_of(dest * feat, HEAD_DIM), feat)

    def seq_copy(a, dest, src):
        hbm, buf = seq_pairs[a]
        return pltpu.make_async_remote_copy(
            src_ref=hbm.at[0, :, seq_lanes(dest)], dst_ref=buf.at[src],
            send_sem=seq_send.at[a, dest], recv_sem=seq_recv.at[a, src],
            device_id=(grp, dest), device_id_type=MESH,
        )

    def keep_copy(a):
        hbm, buf = seq_pairs[a]
        return pltpu.make_async_copy(
            hbm.at[0, :, seq_lanes(sp)], buf.at[sp], keep_sem.at[a]
        )

    def o_copy(local, dest, src):
        lanes = pl.ds(pl.multiple_of(local * HEAD_DIM, HEAD_DIM), HEAD_DIM)
        out_lanes = pl.ds(pl.multiple_of(src * feat + local * HEAD_DIM, HEAD_DIM), HEAD_DIM)
        return pltpu.make_async_remote_copy(
            src_ref=o_buf.at[dest, :, lanes], dst_ref=out_hbm.at[0, :, out_lanes],
            send_sem=o_send.at[local, dest], recv_sem=o_recv.at[local, src],
            device_id=(grp, dest), device_id_type=MESH,
        )

    def o_here(local):
        lanes = pl.ds(pl.multiple_of(local * HEAD_DIM, HEAD_DIM), HEAD_DIM)
        out_lanes = pl.ds(pl.multiple_of(sp * feat + local * HEAD_DIM, HEAD_DIM), HEAD_DIM)
        return pltpu.make_async_copy(
            o_buf.at[sp, :, lanes], out_hbm.at[0, :, out_lanes], o_keep.at[local]
        )

    def loop(count, body):
        def step(i, carry):
            body(i)
            return carry
        lax.fori_loop(0, count, step, 0)

    x_ahead, ends_ahead = 8, 6
    seq_copies = 3 * (n_sp - 1)
    per_step = -(-seq_copies // 9)

    @functools.partial(loop, x_ahead)
    def _(c):
        x_copy(c).start()

    wanted = [owner_ref[ids_ref[lev * PAIR + side]] for lev in range(levels)]
    here = ids_ref[grp]
    my_row = owner_ref[here]
    live = lens_ref[here]

    def level_rows(c):
        own, other = own_buf[c], x_buf[c]
        return [lax.select(side == k, own, other) for k in range(PAIR)]

    def send_own(at, c):
        way, ahead = (0, at + 1) if at == 0 else (1, at - 1)
        own = ref_hbm.at[0, :, :, lanes_of(c)]
        line_copy(way, side, c, own, ahead).start()

    def send_other(at, c):
        way, ahead = (0, at + 1) if at == 0 else (1, at - 1)
        x_copy(c).wait_recv()
        line_copy(way, 1 - side, c, x_buf.at[c], ahead).start()

    for at in (0, levels - 1):
        @pl.when(level == at)
        def _(at=at):
            send_own(at, 0)

    @functools.partial(loop, heads)
    def _(c):
        own_copy(c).start()

    for a in range(3):
        keep_copy(a).start()

    for at in (0, levels - 1):
        @pl.when(level == at)
        def _(at=at):
            @functools.partial(loop, ends_ahead)
            def _(c):
                send_other(at, c)
                send_own(at, c + 1)

    def place(way, lev):
        return lev if way == 0 else levels - 1 - lev

    def relay(at, way, c):
        p = place(way, at)
        ahead = at + 1 if way == 0 else at - 1
        for slot in range(slots_on(p - 1, levels)):
            line_copy(way, slot, c, x_buf.at[c], at).wait_recv()
        if p == levels - 1:
            return
        count = slots_on(p, levels)
        if sends_rows(p, levels):
            for slot in range(PAIR * p):
                line_copy(way, slot, c, line_in.at[way, slot, c], ahead).start()
            line_copy(way, PAIR * p + side, c, own_buf.at[c], ahead).start()
            line_copy(way, PAIR * p + 1 - side, c, x_buf.at[c], ahead).start()
            return
        rows = level_rows(c)
        for slot in range(count):
            row = wanted[place(way, p + 1 + slot)]
            value = pick(line_options(at, way, c, row, slot + 1, rows))
            line_out[way, slot, c] = value
            line_copy(way, slot, c, line_out.at[way, slot, c], ahead).start()

    def line_options(at, way, c, row, slot, rows):
        p = place(way, at)
        options = [(row == at * PAIR + k, rows[k]) for k in range(PAIR)]
        if p == 0:
            return options
        if sends_rows(p - 1, levels):
            return options + [
                (row == place(way, q) * PAIR + k, line_in[way, PAIR * q + k, c])
                for q in range(p) for k in range(PAIR)
            ]
        return options + [(row // PAIR < at if way == 0 else row // PAIR > at, line_in[way, slot, c])]

    def final(at, c):
        rows = level_rows(c)
        options = line_options(at, 0, c, my_row, 0, rows)
        options = options + line_options(at, 1, c, my_row, 0, rows)[PAIR:]
        value = pick(options)
        dest, local = head_of(c)

        @pl.when(dest == sp)
        def _():
            ref_kv[local, sp] = value

        @pl.when(dest != sp)
        def _():
            routed[c] = value
            ref_copy(c, dest, local, sp).start()

    def attend(local, block):
        lanes = pl.ds(pl.multiple_of(local * HEAD_DIM, HEAD_DIM), HEAD_DIM)
        own_keys, ref_keys = n_sp * tokens, n_sp * ref_tokens
        q = q_buf[block, :, lanes]
        k = k_buf[:, :, lanes].reshape(own_keys, HEAD_DIM)
        v = v_buf[:, :, lanes].reshape(own_keys, HEAD_DIM)
        ref_k = ref_kv[local, :, 0].reshape(ref_keys, HEAD_DIM)
        ref_v = ref_kv[local, :, 1].reshape(ref_keys, HEAD_DIM)
        contract = (((1,), (1,)), ((), ()))
        scale = HEAD_DIM ** -0.5
        s_own = lax.dot_general(q, k, contract, preferred_element_type=jnp.float32) * scale
        s_ref = lax.dot_general(q, ref_k, contract, preferred_element_type=jnp.float32) * scale
        col = lax.broadcasted_iota(jnp.int32, s_ref.shape, 1)
        s_ref = jnp.where(col < live, s_ref, -jnp.inf)
        peak = jnp.maximum(
            jnp.max(s_own, axis=1, keepdims=True), jnp.max(s_ref, axis=1, keepdims=True)
        )
        w_own = jnp.exp(s_own - peak)
        w_ref = jnp.exp(s_ref - peak)
        total = jnp.sum(w_own, axis=1, keepdims=True) + jnp.sum(w_ref, axis=1, keepdims=True)
        mixed = jnp.dot(w_own.astype(jnp.bfloat16), v, preferred_element_type=jnp.float32)
        mixed += jnp.dot(w_ref.astype(jnp.bfloat16), ref_v, preferred_element_type=jnp.float32)
        return (mixed / total).astype(jnp.bfloat16)

    last_lag = levels
    units = per_dev * n_sp
    at_once = 2
    per_head = n_sp // at_once
    last_start = heads - 1 + last_lag
    first_unit = max(
        [3 * heads // 4]
        + [(n + 1) * n_sp - 1 + last_lag - n * per_head for n in range(per_dev - 1)]
    )

    @functools.partial(loop, last_start + per_head)
    def _(i):
        @pl.when(i + x_ahead < heads)
        def _():
            x_copy(i + x_ahead).start()

        @pl.when(jnp.logical_and(inner, i < heads))
        def _():
            x_copy(i).wait_recv()

        @pl.when(i < heads)
        def _():
            own_copy(i).wait()

        for at in range(levels):
            @pl.when(level == at)
            def _(at=at):
                if at in (0, levels - 1):
                    @pl.when(i + ends_ahead < heads)
                    def _():
                        send_other(at, i + ends_ahead)

                    @pl.when(i + ends_ahead + 1 < heads)
                    def _():
                        send_own(at, i + ends_ahead + 1)

                for p, way in sorted((place(way, at), way) for way in (0, 1)):
                    if p == 0:
                        continue
                    c = i - (0 if p == 1 else p + 1)

                    @pl.when(jnp.logical_and(c >= 0, c < heads))
                    def _(c=c, way=way):
                        relay(at, way, c)

                done = i - last_lag

                @pl.when(jnp.logical_and(done >= 0, done < heads))
                def _():
                    final(at, done)

        for n in range(per_step):
            number = i * per_step + n

            @pl.when(number < seq_copies)
            def _(number=number):
                dest = (sp + 1 + number // 3) % n_sp
                for a in range(3):
                    @pl.when(number % 3 == a)
                    def _(a=a):
                        seq_copy(a, dest, sp).start()

        early = (i - first_unit) * at_once
        late = (i - last_start) * at_once + units - n_sp
        unit = jnp.where(i >= last_start, late, early)
        due = jnp.logical_or(
            jnp.logical_and(early >= 0, early < units - n_sp), i >= last_start
        )

        @pl.when(due)
        def _():
            local, turn = unit // n_sp, unit % n_sp

            @pl.when(unit == 0)
            def _():
                for a in range(3):
                    keep_copy(a).wait()

                @functools.partial(loop, n_sp - 1)
                def _(step):
                    src = (sp + 1 + step) % n_sp
                    for a in range(3):
                        seq_copy(a, sp, src).wait_recv()

            @pl.when(turn == 0)
            def _():
                @functools.partial(loop, n_sp - 1)
                def _(step):
                    src = (sp + 1 + step) % n_sp
                    ref_copy(0, sp, local, src).wait_recv()

            lanes = pl.ds(pl.multiple_of(local * HEAD_DIM, HEAD_DIM), HEAD_DIM)
            blocks = [(sp + 1 + turn + n) % n_sp for n in range(at_once)]
            results = [attend(local, block) for block in blocks]
            for block, result in zip(blocks, results):
                o_buf[block, :, lanes] = result
            for block in blocks:
                @pl.when(block == sp)
                def _():
                    o_here(local).start()

                @pl.when(block != sp)
                def _(block=block):
                    o_copy(local, block, sp).start()

    @functools.partial(loop, heads)
    def _(c):
        x_copy(c).wait_send()
        dest, local = head_of(c)

        @pl.when(dest != sp)
        def _():
            ref_copy(c, dest, local, sp).wait_send()

        for at in range(levels):
            @pl.when(level == at)
            def _(at=at):
                for way in (0, 1):
                    p = place(way, at)
                    if p < levels - 1:
                        for slot in range(slots_on(p, levels)):
                            line_copy(way, slot, c, x_buf.at[c], at).wait_send()

    @functools.partial(loop, n_sp - 1)
    def _(step):
        other = (sp + 1 + step) % n_sp
        for a in range(3):
            seq_copy(a, other, sp).wait_send()
        for local in range(per_dev):
            o_copy(local, other, sp).wait_send()
            o_copy(local, sp, other).wait_recv()

    for local in range(per_dev):
        o_here(local).wait()


def shards(n_grp, n_sp, queries, keys, values, ref_cache, ref_ids, ref_owner, ref_lens):
    tokens, width = queries.shape[1:]
    ref_tokens = ref_cache.shape[2]
    heads = width // HEAD_DIM
    per_dev = heads // n_sp
    feat = per_dev * HEAD_DIM
    levels = n_grp // PAIR
    slots = max(slots_on(p, levels) for p in range(levels - 1))
    chunk = (2, ref_tokens, HEAD_DIM)
    bf16 = jnp.bfloat16
    dma = pltpu.SemaphoreType.DMA
    smem = pl.BlockSpec(memory_space=pltpu.SMEM)
    hbm = pl.BlockSpec(memory_space=pl.ANY)
    all_keys = n_sp * (tokens + ref_tokens)
    return pl.pallas_call(
        functools.partial(kernel, n_grp, n_sp),
        out_shape=jax.ShapeDtypeStruct(queries.shape, bf16),
        in_specs=[smem] * 3 + [hbm] * 4,
        out_specs=hbm,
        scratch_shapes=[
            pltpu.VMEM((n_sp, tokens, feat), bf16),
            pltpu.VMEM((n_sp, tokens, feat), bf16),
            pltpu.VMEM((n_sp, tokens, feat), bf16),
            pltpu.VMEM((heads,) + chunk, bf16),
            pltpu.VMEM((heads,) + chunk, bf16),
            pltpu.VMEM((2, slots, heads) + chunk, bf16),
            pltpu.VMEM((2, slots, heads) + chunk, bf16),
            pltpu.VMEM((heads,) + chunk, bf16),
            pltpu.VMEM((per_dev, n_sp) + chunk, bf16),
            pltpu.VMEM((n_sp, tokens, feat), bf16),
            dma((heads,)),
            dma((3,)),
            dma((3, n_sp)),
            dma((3, n_sp)),
            dma((heads,)),
            dma((heads,)),
            dma((2, slots, heads)),
            dma((2, slots, heads)),
            dma((heads,)),
            dma((per_dev, n_sp)),
            dma((per_dev,)),
            dma((per_dev, n_sp)),
            dma((per_dev, n_sp)),
        ],
        compiler_params=pltpu.CompilerParams(
            collective_id=0, has_side_effects=True, vmem_limit_bytes=60 * 1024 * 1024
        ),
        cost_estimate=pl.CostEstimate(
            flops=4 * n_sp * tokens * all_keys * feat,
            bytes_accessed=8 * tokens * width * 2,
            transcendentals=per_dev * n_sp * tokens * all_keys,
        ),
    )(ref_ids, ref_owner, ref_lens, queries, keys, values, ref_cache)


def solution(mesh):
    in_specs = (
        P("grp", "sp", None),
        P("grp", "sp", None),
        P("grp", "sp", None),
        P("grp", None, "sp", None),
        P(),
        P(),
        P(),
    )
    body = functools.partial(shards, mesh.shape["grp"], mesh.shape["sp"])
    return jax.shard_map(
        body, mesh=mesh, in_specs=in_specs, out_specs=P("grp", "sp", None), check_vma=False
    )
```

```python
import functools

import jax
import jax.numpy as jnp
from jax import lax
from jax.experimental import pallas as pl
from jax.experimental.pallas import tpu as pltpu
from jax.sharding import PartitionSpec as P

HEAD_DIM = 128
PAIR = 2
MESH = pl.DeviceIdType.MESH


def slots_on(p, levels):
    return min(PAIR * (p + 1), levels - 1 - p)


def sends_rows(p, levels):
    return PAIR * (p + 1) <= levels - 1 - p


def pick(options):
    value = options[-1][1]
    for cond, other in reversed(options[:-1]):
        value = lax.select(cond, other, value)
    return value


def kernel(
    n_grp, n_sp,
    ids_ref, owner_ref, lens_ref, q_hbm, k_hbm, v_hbm, ref_hbm, out_hbm,
    q_buf, k_buf, v_buf, q_stage, k_stage, v_stage, own_buf, x_buf, line_in, line_out, routed, ref_kv, o_buf,
    own_sem, keep_sem, stage_sem, seq_send, seq_recv, x_send, x_recv, line_send, line_recv,
    ref_send, ref_recv, o_keep, o_send, o_recv,
):
    levels = n_grp // PAIR
    heads = ref_hbm.shape[-1] // HEAD_DIM
    per_dev = heads // n_sp
    feat = per_dev * HEAD_DIM
    tokens = q_hbm.shape[1]
    ref_tokens = ref_hbm.shape[2]
    grp = lax.axis_index("grp")
    sp = lax.axis_index("sp")
    level = grp // PAIR
    side = grp % PAIR
    mate = level * PAIR + (1 - side)

    def at_level(other):
        return (other * PAIR + side, sp)

    def head_of(c):
        return (c + sp) % n_sp, c // n_sp

    def lanes_of(c):
        dest, local = head_of(c)
        return pl.ds(pl.multiple_of((dest * per_dev + local) * HEAD_DIM, HEAD_DIM), HEAD_DIM)

    def own_copy(c):
        return pltpu.make_async_copy(
            ref_hbm.at[0, :, :, lanes_of(c)], own_buf.at[c], own_sem.at[c]
        )

    def x_copy(c):
        return pltpu.make_async_remote_copy(
            src_ref=own_buf.at[c], dst_ref=x_buf.at[c],
            send_sem=x_send.at[c], recv_sem=x_recv.at[c],
            device_id=(mate, sp), device_id_type=MESH,
        )

    def line_copy(way, slot, c, src, other):
        return pltpu.make_async_remote_copy(
            src_ref=src, dst_ref=line_in.at[way, slot, c],
            send_sem=line_send.at[way, slot, c], recv_sem=line_recv.at[way, slot, c],
            device_id=at_level(other), device_id_type=MESH,
        )

    def ref_copy(c, dest, local, src):
        return pltpu.make_async_remote_copy(
            src_ref=routed.at[c], dst_ref=ref_kv.at[local, src],
            send_sem=ref_send.at[c], recv_sem=ref_recv.at[local, src],
            device_id=(grp, dest), device_id_type=MESH,
        )

    seq_refs = (
        (q_hbm, q_stage, q_buf), (k_hbm, k_stage, k_buf), (v_hbm, v_stage, v_buf)
    )

    def seq_lanes(dest):
        return pl.ds(pl.multiple_of(dest * feat, HEAD_DIM), feat)

    def seq_copy(a, dest, src):
        _, stage, buf = seq_refs[a]
        return pltpu.make_async_remote_copy(
            src_ref=stage.at[dest], dst_ref=buf.at[src],
            send_sem=seq_send.at[a, dest], recv_sem=seq_recv.at[a, src],
            device_id=(grp, dest), device_id_type=MESH,
        )

    def keep_copy(a):
        hbm, _, buf = seq_refs[a]
        return pltpu.make_async_copy(
            hbm.at[0, :, seq_lanes(sp)], buf.at[sp], keep_sem.at[a]
        )

    def stage_copy(a, dest):
        hbm, stage, _ = seq_refs[a]
        return pltpu.make_async_copy(
            hbm.at[0, :, seq_lanes(dest)], stage.at[dest], stage_sem.at[a, dest]
        )

    def o_copy(local, dest, src):
        lanes = pl.ds(pl.multiple_of(local * HEAD_DIM, HEAD_DIM), HEAD_DIM)
        out_lanes = pl.ds(pl.multiple_of(src * feat + local * HEAD_DIM, HEAD_DIM), HEAD_DIM)
        return pltpu.make_async_remote_copy(
            src_ref=o_buf.at[dest, :, lanes], dst_ref=out_hbm.at[0, :, out_lanes],
            send_sem=o_send.at[local, dest], recv_sem=o_recv.at[local, src],
            device_id=(grp, dest), device_id_type=MESH,
        )

    def o_here(local):
        lanes = pl.ds(pl.multiple_of(local * HEAD_DIM, HEAD_DIM), HEAD_DIM)
        out_lanes = pl.ds(pl.multiple_of(sp * feat + local * HEAD_DIM, HEAD_DIM), HEAD_DIM)
        return pltpu.make_async_copy(
            o_buf.at[sp, :, lanes], out_hbm.at[0, :, out_lanes], o_keep.at[local]
        )

    def loop(count, body):
        def step(i, carry):
            body(i)
            return carry
        lax.fori_loop(0, count, step, 0)

    x_ahead, ends_ahead = 8, 6
    seq_copies = 3 * (n_sp - 1)
    per_step = -(-seq_copies // 9)

    inner = jnp.logical_and(level > 0, level < levels - 1)

    @functools.partial(loop, heads)
    def _(c):
        own_copy(c).start()

    @functools.partial(loop, n_sp - 1)
    def _(step):
        for a in range(3):
            stage_copy(a, (sp + 1 + step) % n_sp).start()

    for a in range(3):
        keep_copy(a).start()

    barrier = pltpu.get_barrier_semaphore()

    def greet(device):
        pl.semaphore_signal(barrier, inc=1, device_id=device, device_id_type=MESH)

    greet((mate, sp))
    for step in range(1, n_sp):
        greet((grp, (sp + step) % n_sp))

    @pl.when(level > 0)
    def _():
        greet(at_level(level - 1))

    @pl.when(level < levels - 1)
    def _():
        greet(at_level(level + 1))

    pl.semaphore_wait(barrier, n_sp + 1 + inner.astype(jnp.int32))

    @functools.partial(loop, heads)
    def _(c):
        own_copy(c).wait()

    @functools.partial(loop, x_ahead)
    def _(c):
        x_copy(c).start()

    wanted = [owner_ref[ids_ref[lev * PAIR + side]] for lev in range(levels)]
    here = ids_ref[grp]
    my_row = owner_ref[here]
    live = lens_ref[here]

    def level_rows(c):
        own, other = own_buf[c], x_buf[c]
        return [lax.select(side == k, own, other) for k in range(PAIR)]

    def send_own(at, c):
        way, ahead = (0, at + 1) if at == 0 else (1, at - 1)
        line_copy(way, side, c, own_buf.at[c], ahead).start()

    def send_other(at, c):
        way, ahead = (0, at + 1) if at == 0 else (1, at - 1)
        x_copy(c).wait_recv()
        line_copy(way, 1 - side, c, x_buf.at[c], ahead).start()

    for at in (0, levels - 1):
        @pl.when(level == at)
        def _(at=at):
            send_own(at, 0)

            @functools.partial(loop, ends_ahead)
            def _(c):
                send_other(at, c)
                send_own(at, c + 1)

    def place(way, lev):
        return lev if way == 0 else levels - 1 - lev

    def relay(at, way, c):
        p = place(way, at)
        ahead = at + 1 if way == 0 else at - 1
        for slot in range(slots_on(p - 1, levels)):
            line_copy(way, slot, c, x_buf.at[c], at).wait_recv()
        if p == levels - 1:
            return
        count = slots_on(p, levels)
        if sends_rows(p, levels):
            for slot in range(PAIR * p):
                line_copy(way, slot, c, line_in.at[way, slot, c], ahead).start()
            line_copy(way, PAIR * p + side, c, own_buf.at[c], ahead).start()
            line_copy(way, PAIR * p + 1 - side, c, x_buf.at[c], ahead).start()
            return
        rows = level_rows(c)
        for slot in range(count):
            row = wanted[place(way, p + 1 + slot)]
            value = pick(line_options(at, way, c, row, slot + 1, rows))
            line_out[way, slot, c] = value
            line_copy(way, slot, c, line_out.at[way, slot, c], ahead).start()

    def line_options(at, way, c, row, slot, rows):
        p = place(way, at)
        options = [(row == at * PAIR + k, rows[k]) for k in range(PAIR)]
        if p == 0:
            return options
        if sends_rows(p - 1, levels):
            return options + [
                (row == place(way, q) * PAIR + k, line_in[way, PAIR * q + k, c])
                for q in range(p) for k in range(PAIR)
            ]
        return options + [(row // PAIR < at if way == 0 else row // PAIR > at, line_in[way, slot, c])]

    def final(at, c):
        rows = level_rows(c)
        options = line_options(at, 0, c, my_row, 0, rows)
        options = options + line_options(at, 1, c, my_row, 0, rows)[PAIR:]
        value = pick(options)
        dest, local = head_of(c)

        @pl.when(dest == sp)
        def _():
            ref_kv[local, sp] = value

        @pl.when(dest != sp)
        def _():
            routed[c] = value
            ref_copy(c, dest, local, sp).start()

    def attend(local, block):
        lanes = pl.ds(pl.multiple_of(local * HEAD_DIM, HEAD_DIM), HEAD_DIM)
        own_keys, ref_keys = n_sp * tokens, n_sp * ref_tokens
        q = q_buf[block, :, lanes]
        k = k_buf[:, :, lanes].reshape(own_keys, HEAD_DIM)
        v = v_buf[:, :, lanes].reshape(own_keys, HEAD_DIM)
        ref_k = ref_kv[local, :, 0].reshape(ref_keys, HEAD_DIM)
        ref_v = ref_kv[local, :, 1].reshape(ref_keys, HEAD_DIM)
        contract = (((1,), (1,)), ((), ()))
        scale = HEAD_DIM ** -0.5
        s_own = lax.dot_general(q, k, contract, preferred_element_type=jnp.float32) * scale
        s_ref = lax.dot_general(q, ref_k, contract, preferred_element_type=jnp.float32) * scale
        col = lax.broadcasted_iota(jnp.int32, s_ref.shape, 1)
        s_ref = jnp.where(col < live, s_ref, -jnp.inf)
        peak = jnp.maximum(
            jnp.max(s_own, axis=1, keepdims=True), jnp.max(s_ref, axis=1, keepdims=True)
        )
        w_own = jnp.exp(s_own - peak)
        w_ref = jnp.exp(s_ref - peak)
        total = jnp.sum(w_own, axis=1, keepdims=True) + jnp.sum(w_ref, axis=1, keepdims=True)
        mixed = jnp.dot(w_own.astype(jnp.bfloat16), v, preferred_element_type=jnp.float32)
        mixed += jnp.dot(w_ref.astype(jnp.bfloat16), ref_v, preferred_element_type=jnp.float32)
        return (mixed / total).astype(jnp.bfloat16)

    last_lag = levels
    units = per_dev * n_sp
    at_once = 2
    per_head = n_sp // at_once
    last_start = heads - 1 + last_lag
    first_unit = max(
        [3 * heads // 4]
        + [(n + 1) * n_sp - 1 + last_lag - n * per_head for n in range(per_dev - 1)]
    )

    @functools.partial(loop, last_start + per_head)
    def _(i):
        @pl.when(i + x_ahead < heads)
        def _():
            x_copy(i + x_ahead).start()

        @pl.when(jnp.logical_and(inner, i < heads))
        def _():
            x_copy(i).wait_recv()

        for at in range(levels):
            @pl.when(level == at)
            def _(at=at):
                if at in (0, levels - 1):
                    @pl.when(i + ends_ahead < heads)
                    def _():
                        send_other(at, i + ends_ahead)

                    @pl.when(i + ends_ahead + 1 < heads)
                    def _():
                        send_own(at, i + ends_ahead + 1)

                for p, way in sorted((place(way, at), way) for way in (0, 1)):
                    if p == 0:
                        continue
                    c = i - (0 if p == 1 else p + 1)

                    @pl.when(jnp.logical_and(c >= 0, c < heads))
                    def _(c=c, way=way):
                        relay(at, way, c)

                done = i - last_lag

                @pl.when(jnp.logical_and(done >= 0, done < heads))
                def _():
                    final(at, done)

        for n in range(per_step):
            number = i * per_step + n

            @pl.when(number < seq_copies)
            def _(number=number):
                dest = (sp + 1 + number // 3) % n_sp
                for a in range(3):
                    @pl.when(number % 3 == a)
                    def _(a=a):
                        stage_copy(a, dest).wait()
                        seq_copy(a, dest, sp).start()

        early = (i - first_unit) * at_once
        late = (i - last_start) * at_once + units - n_sp
        unit = jnp.where(i >= last_start, late, early)
        due = jnp.logical_or(
            jnp.logical_and(early >= 0, early < units - n_sp), i >= last_start
        )

        @pl.when(due)
        def _():
            local, turn = unit // n_sp, unit % n_sp

            @pl.when(unit == 0)
            def _():
                for a in range(3):
                    keep_copy(a).wait()

                @functools.partial(loop, n_sp - 1)
                def _(step):
                    src = (sp + 1 + step) % n_sp
                    for a in range(3):
                        seq_copy(a, sp, src).wait_recv()

            @pl.when(turn == 0)
            def _():
                @functools.partial(loop, n_sp - 1)
                def _(step):
                    src = (sp + 1 + step) % n_sp
                    ref_copy(0, sp, local, src).wait_recv()

            lanes = pl.ds(pl.multiple_of(local * HEAD_DIM, HEAD_DIM), HEAD_DIM)
            blocks = [(sp + 1 + turn + n) % n_sp for n in range(at_once)]
            results = [attend(local, block) for block in blocks]
            for block, result in zip(blocks, results):
                o_buf[block, :, lanes] = result
            for block in blocks:
                @pl.when(block == sp)
                def _():
                    o_here(local).start()

                @pl.when(block != sp)
                def _(block=block):
                    o_copy(local, block, sp).start()

    @functools.partial(loop, heads)
    def _(c):
        x_copy(c).wait_send()
        dest, local = head_of(c)

        @pl.when(dest != sp)
        def _():
            ref_copy(c, dest, local, sp).wait_send()

        for at in range(levels):
            @pl.when(level == at)
            def _(at=at):
                for way in (0, 1):
                    p = place(way, at)
                    if p < levels - 1:
                        for slot in range(slots_on(p, levels)):
                            line_copy(way, slot, c, x_buf.at[c], at).wait_send()

    @functools.partial(loop, n_sp - 1)
    def _(step):
        other = (sp + 1 + step) % n_sp
        for a in range(3):
            seq_copy(a, other, sp).wait_send()
        for local in range(per_dev):
            o_copy(local, other, sp).wait_send()
            o_copy(local, sp, other).wait_recv()

    for local in range(per_dev):
        o_here(local).wait()


def shards(n_grp, n_sp, queries, keys, values, ref_cache, ref_ids, ref_owner, ref_lens):
    tokens, width = queries.shape[1:]
    ref_tokens = ref_cache.shape[2]
    heads = width // HEAD_DIM
    per_dev = heads // n_sp
    feat = per_dev * HEAD_DIM
    levels = n_grp // PAIR
    slots = max(slots_on(p, levels) for p in range(levels - 1))
    chunk = (2, ref_tokens, HEAD_DIM)
    bf16 = jnp.bfloat16
    dma = pltpu.SemaphoreType.DMA
    smem = pl.BlockSpec(memory_space=pltpu.SMEM)
    hbm = pl.BlockSpec(memory_space=pl.ANY)
    all_keys = n_sp * (tokens + ref_tokens)
    return pl.pallas_call(
        functools.partial(kernel, n_grp, n_sp),
        out_shape=jax.ShapeDtypeStruct(queries.shape, bf16),
        in_specs=[smem] * 3 + [hbm] * 4,
        out_specs=hbm,
        scratch_shapes=[
            pltpu.VMEM((n_sp, tokens, feat), bf16),
            pltpu.VMEM((n_sp, tokens, feat), bf16),
            pltpu.VMEM((n_sp, tokens, feat), bf16),
            pltpu.VMEM((n_sp, tokens, feat), bf16),
            pltpu.VMEM((n_sp, tokens, feat), bf16),
            pltpu.VMEM((n_sp, tokens, feat), bf16),
            pltpu.VMEM((heads,) + chunk, bf16),
            pltpu.VMEM((heads,) + chunk, bf16),
            pltpu.VMEM((2, slots, heads) + chunk, bf16),
            pltpu.VMEM((2, slots, heads) + chunk, bf16),
            pltpu.VMEM((heads,) + chunk, bf16),
            pltpu.VMEM((per_dev, n_sp) + chunk, bf16),
            pltpu.VMEM((n_sp, tokens, feat), bf16),
            dma((heads,)),
            dma((3,)),
            dma((3, n_sp)),
            dma((3, n_sp)),
            dma((3, n_sp)),
            dma((heads,)),
            dma((heads,)),
            dma((2, slots, heads)),
            dma((2, slots, heads)),
            dma((heads,)),
            dma((per_dev, n_sp)),
            dma((per_dev,)),
            dma((per_dev, n_sp)),
            dma((per_dev, n_sp)),
        ],
        compiler_params=pltpu.CompilerParams(
            collective_id=0, has_side_effects=True, vmem_limit_bytes=60 * 1024 * 1024
        ),
        cost_estimate=pl.CostEstimate(
            flops=4 * n_sp * tokens * all_keys * feat,
            bytes_accessed=8 * tokens * width * 2,
            transcendentals=per_dev * n_sp * tokens * all_keys,
        ),
    )(ref_ids, ref_owner, ref_lens, queries, keys, values, ref_cache)


def solution(mesh):
    in_specs = (
        P("grp", "sp", None),
        P("grp", "sp", None),
        P("grp", "sp", None),
        P("grp", None, "sp", None),
        P(),
        P(),
        P(),
    )
    body = functools.partial(shards, mesh.shape["grp"], mesh.shape["sp"])
    return jax.shard_map(
        body, mesh=mesh, in_specs=in_specs, out_specs=P("grp", "sp", None), check_vma=False
    )
```

```python
import functools

import jax
import jax.numpy as jnp
from jax import lax
from jax.experimental import pallas as pl
from jax.experimental.pallas import tpu as pltpu
from jax.sharding import PartitionSpec as P

HEAD_DIM = 128
PAIR = 2
MESH = pl.DeviceIdType.MESH


def slots_on(p, levels):
    return min(PAIR * (p + 1), levels - 1 - p)


def sends_rows(p, levels):
    return PAIR * (p + 1) <= levels - 1 - p


def pick(options):
    value = options[-1][1]
    for cond, other in reversed(options[:-1]):
        value = lax.select(cond, other, value)
    return value


def kernel(
    n_grp, n_sp,
    ids_ref, owner_ref, lens_ref, q_hbm, k_hbm, v_hbm, ref_hbm, out_hbm,
    q_buf, k_buf, v_buf, q_stage, k_stage, v_stage, own_buf, x_buf, line_in, line_out, routed, ref_kv, o_buf,
    own_sem, keep_sem, stage_sem, seq_send, seq_recv, x_send, x_recv, line_send, line_recv,
    ref_send, ref_recv, o_keep, o_send, o_recv,
):
    levels = n_grp // PAIR
    heads = ref_hbm.shape[-1] // HEAD_DIM
    per_dev = heads // n_sp
    feat = per_dev * HEAD_DIM
    tokens = q_hbm.shape[1]
    ref_tokens = ref_hbm.shape[2]
    grp = lax.axis_index("grp")
    sp = lax.axis_index("sp")
    level = grp // PAIR
    side = grp % PAIR
    mate = level * PAIR + (1 - side)

    def at_level(other):
        return (other * PAIR + side, sp)

    chunks = 2 * heads

    def head_of(c):
        return (c // 2 + sp) % n_sp, c // (2 * n_sp)

    def turn_of(step):
        return (sp // 2 * 2 + 2 + step) % n_sp

    def lanes_of(c):
        dest, local = head_of(c)
        return pl.ds(pl.multiple_of((dest * per_dev + local) * HEAD_DIM, HEAD_DIM), HEAD_DIM)

    def own_copy(c):
        return pltpu.make_async_copy(
            ref_hbm.at[0, c % 2, :, lanes_of(c)], own_buf.at[c], own_sem.at[c]
        )

    def x_copy(c):
        return pltpu.make_async_remote_copy(
            src_ref=own_buf.at[c], dst_ref=x_buf.at[c],
            send_sem=x_send.at[c], recv_sem=x_recv.at[c],
            device_id=(mate, sp), device_id_type=MESH,
        )

    def line_copy(way, slot, c, src, other):
        return pltpu.make_async_remote_copy(
            src_ref=src, dst_ref=line_in.at[way, slot, c],
            send_sem=line_send.at[way, slot, c], recv_sem=line_recv.at[way, slot, c],
            device_id=at_level(other), device_id_type=MESH,
        )

    def ref_copy(c, dest, local, src):
        half = c % 2
        return pltpu.make_async_remote_copy(
            src_ref=routed.at[c], dst_ref=ref_kv.at[local, half, src],
            send_sem=ref_send.at[c], recv_sem=ref_recv.at[local, half, src],
            device_id=(grp, dest), device_id_type=MESH,
        )

    seq_refs = (
        (q_hbm, q_stage, q_buf), (k_hbm, k_stage, k_buf), (v_hbm, v_stage, v_buf)
    )

    def seq_lanes(dest):
        return pl.ds(pl.multiple_of(dest * feat, HEAD_DIM), feat)

    def seq_copy(a, dest, src):
        _, stage, buf = seq_refs[a]
        return pltpu.make_async_remote_copy(
            src_ref=stage.at[dest], dst_ref=buf.at[src],
            send_sem=seq_send.at[a, dest], recv_sem=seq_recv.at[a, src],
            device_id=(grp, dest), device_id_type=MESH,
        )

    def keep_copy(a):
        hbm, _, buf = seq_refs[a]
        return pltpu.make_async_copy(
            hbm.at[0, :, seq_lanes(sp)], buf.at[sp], keep_sem.at[a]
        )

    def stage_copy(a, dest):
        hbm, stage, _ = seq_refs[a]
        return pltpu.make_async_copy(
            hbm.at[0, :, seq_lanes(dest)], stage.at[dest], stage_sem.at[a, dest]
        )

    def o_copy(local, dest, src):
        lanes = pl.ds(pl.multiple_of(local * HEAD_DIM, HEAD_DIM), HEAD_DIM)
        out_lanes = pl.ds(pl.multiple_of(src * feat + local * HEAD_DIM, HEAD_DIM), HEAD_DIM)
        return pltpu.make_async_remote_copy(
            src_ref=o_buf.at[dest, :, lanes], dst_ref=out_hbm.at[0, :, out_lanes],
            send_sem=o_send.at[local, dest], recv_sem=o_recv.at[local, src],
            device_id=(grp, dest), device_id_type=MESH,
        )

    def o_here(local):
        lanes = pl.ds(pl.multiple_of(local * HEAD_DIM, HEAD_DIM), HEAD_DIM)
        out_lanes = pl.ds(pl.multiple_of(sp * feat + local * HEAD_DIM, HEAD_DIM), HEAD_DIM)
        return pltpu.make_async_copy(
            o_buf.at[sp, :, lanes], out_hbm.at[0, :, out_lanes], o_keep.at[local]
        )

    def loop(count, body):
        def step(i, carry):
            body(i)
            return carry
        lax.fori_loop(0, count, step, 0)

    x_ahead, ends_ahead = 13, 10
    seq_copies = 3 * n_sp
    per_step = -(-seq_copies // 12)

    inner = jnp.logical_and(level > 0, level < levels - 1)

    @functools.partial(loop, chunks)
    def _(c):
        own_copy(c).start()

    @functools.partial(loop, n_sp - 1)
    def _(step):
        for a in range(3):
            stage_copy(a, (sp + 1 + step) % n_sp).start()

    for a in range(3):
        keep_copy(a).start()

    barrier = pltpu.get_barrier_semaphore()

    def greet(device):
        pl.semaphore_signal(barrier, inc=1, device_id=device, device_id_type=MESH)

    greet((mate, sp))
    for step in range(1, n_sp):
        greet((grp, (sp + step) % n_sp))

    @pl.when(level > 0)
    def _():
        greet(at_level(level - 1))

    @pl.when(level < levels - 1)
    def _():
        greet(at_level(level + 1))

    pl.semaphore_wait(barrier, n_sp + 1 + inner.astype(jnp.int32))

    @functools.partial(loop, chunks)
    def _(c):
        own_copy(c).wait()

    @functools.partial(loop, x_ahead)
    def _(c):
        x_copy(c).start()

    wanted = [owner_ref[ids_ref[lev * PAIR + side]] for lev in range(levels)]
    here = ids_ref[grp]
    my_row = owner_ref[here]
    live = lens_ref[here]

    def level_rows(c):
        own, other = own_buf[c], x_buf[c]
        return [lax.select(side == k, own, other) for k in range(PAIR)]

    def send_own(at, c):
        way, ahead = (0, at + 1) if at == 0 else (1, at - 1)
        line_copy(way, side, c, own_buf.at[c], ahead).start()

    def send_other(at, c):
        way, ahead = (0, at + 1) if at == 0 else (1, at - 1)
        x_copy(c).wait_recv()
        line_copy(way, 1 - side, c, x_buf.at[c], ahead).start()

    for at in (0, levels - 1):
        @pl.when(level == at)
        def _(at=at):
            send_own(at, 0)

            @functools.partial(loop, ends_ahead)
            def _(c):
                send_other(at, c)
                send_own(at, c + 1)

    def place(way, lev):
        return lev if way == 0 else levels - 1 - lev

    def relay(at, way, c):
        p = place(way, at)
        ahead = at + 1 if way == 0 else at - 1
        for slot in range(slots_on(p - 1, levels)):
            line_copy(way, slot, c, x_buf.at[c], at).wait_recv()
        if p == levels - 1:
            return
        count = slots_on(p, levels)
        if sends_rows(p, levels):
            for slot in range(PAIR * p):
                line_copy(way, slot, c, line_in.at[way, slot, c], ahead).start()
            line_copy(way, PAIR * p + side, c, own_buf.at[c], ahead).start()
            line_copy(way, PAIR * p + 1 - side, c, x_buf.at[c], ahead).start()
            return
        rows = level_rows(c)
        for slot in range(count):
            row = wanted[place(way, p + 1 + slot)]
            value = pick(line_options(at, way, c, row, slot + 1, rows))
            line_out[way, slot, c] = value
            line_copy(way, slot, c, line_out.at[way, slot, c], ahead).start()

    def line_options(at, way, c, row, slot, rows):
        p = place(way, at)
        options = [(row == at * PAIR + k, rows[k]) for k in range(PAIR)]
        if p == 0:
            return options
        if sends_rows(p - 1, levels):
            return options + [
                (row == place(way, q) * PAIR + k, line_in[way, PAIR * q + k, c])
                for q in range(p) for k in range(PAIR)
            ]
        return options + [(row // PAIR < at if way == 0 else row // PAIR > at, line_in[way, slot, c])]

    def final(at, c):
        rows = level_rows(c)
        options = line_options(at, 0, c, my_row, 0, rows)
        options = options + line_options(at, 1, c, my_row, 0, rows)[PAIR:]
        value = pick(options)
        dest, local = head_of(c)

        @pl.when(dest == sp)
        def _():
            ref_kv[local, c % 2, sp] = value

        @pl.when(dest != sp)
        def _():
            routed[c] = value
            ref_copy(c, dest, local, sp).start()

    def attend(local, block):
        lanes = pl.ds(pl.multiple_of(local * HEAD_DIM, HEAD_DIM), HEAD_DIM)
        own_keys, ref_keys = n_sp * tokens, n_sp * ref_tokens
        q = q_buf[block, :, lanes]
        k = k_buf[:, :, lanes].reshape(own_keys, HEAD_DIM)
        v = v_buf[:, :, lanes].reshape(own_keys, HEAD_DIM)
        ref_k = ref_kv[local, 0].reshape(ref_keys, HEAD_DIM)
        ref_v = ref_kv[local, 1].reshape(ref_keys, HEAD_DIM)
        contract = (((1,), (1,)), ((), ()))
        scale = HEAD_DIM ** -0.5
        s_own = lax.dot_general(q, k, contract, preferred_element_type=jnp.float32) * scale
        s_ref = lax.dot_general(q, ref_k, contract, preferred_element_type=jnp.float32) * scale
        col = lax.broadcasted_iota(jnp.int32, s_ref.shape, 1)
        s_ref = jnp.where(col < live, s_ref, -jnp.inf)
        peak = jnp.maximum(
            jnp.max(s_own, axis=1, keepdims=True), jnp.max(s_ref, axis=1, keepdims=True)
        )
        w_own = jnp.exp(s_own - peak)
        w_ref = jnp.exp(s_ref - peak)
        total = jnp.sum(w_own, axis=1, keepdims=True) + jnp.sum(w_ref, axis=1, keepdims=True)
        mixed = jnp.dot(w_own.astype(jnp.bfloat16), v, preferred_element_type=jnp.float32)
        mixed += jnp.dot(w_ref.astype(jnp.bfloat16), ref_v, preferred_element_type=jnp.float32)
        return (mixed / total).astype(jnp.bfloat16)

    last_lag = 2 * (levels - 1)
    units = per_dev * n_sp
    at_once = 2
    per_head = n_sp // at_once
    last_start = chunks - 1 + last_lag
    first_unit = max(
        [3 * chunks // 4]
        + [2 * (n + 1) * n_sp - 1 + last_lag - 2 * n * per_head for n in range(per_dev - 1)]
    )

    @functools.partial(loop, last_start + per_head)
    def _(i):
        @pl.when(i + x_ahead < chunks)
        def _():
            x_copy(i + x_ahead).start()

        @pl.when(jnp.logical_and(inner, i < chunks))
        def _():
            x_copy(i).wait_recv()

        for at in range(levels):
            @pl.when(level == at)
            def _(at=at):
                if at in (0, levels - 1):
                    @pl.when(i + ends_ahead < chunks)
                    def _():
                        send_other(at, i + ends_ahead)

                    @pl.when(i + ends_ahead + 1 < chunks)
                    def _():
                        send_own(at, i + ends_ahead + 1)

                for p, way in sorted((place(way, at), way) for way in (0, 1)):
                    if p == 0:
                        continue
                    c = i - (0 if p == 1 else 2 * p)

                    @pl.when(jnp.logical_and(c >= 0, c < chunks))
                    def _(c=c, way=way):
                        relay(at, way, c)

                done = i - last_lag

                @pl.when(jnp.logical_and(done >= 0, done < chunks))
                def _():
                    final(at, done)

        for n in range(per_step):
            number = i // 2 * per_step + n
            dest = turn_of(number // 3)
            start = jnp.logical_and(i % 2 == 0, number < seq_copies)

            @pl.when(jnp.logical_and(start, dest != sp))
            def _(number=number, dest=dest):
                for a in range(3):
                    @pl.when(number % 3 == a)
                    def _(a=a):
                        stage_copy(a, dest).wait()
                        seq_copy(a, dest, sp).start()

        early = (i - first_unit) // 2 * at_once
        late = (i - last_start) * at_once + units - n_sp
        unit = jnp.where(i >= last_start, late, early)
        due = jnp.logical_or(
            jnp.logical_and(
                jnp.logical_and(i >= first_unit, (i - first_unit) % 2 == 0),
                early < units - n_sp,
            ),
            i >= last_start,
        )

        @pl.when(due)
        def _():
            local, turn = unit // n_sp, unit % n_sp

            @pl.when(unit == 0)
            def _():
                for a in range(3):
                    keep_copy(a).wait()

                @functools.partial(loop, n_sp - 1)
                def _(step):
                    src = (sp + 1 + step) % n_sp
                    for a in range(3):
                        seq_copy(a, sp, src).wait_recv()

            @pl.when(turn == 0)
            def _():
                @functools.partial(loop, n_sp - 1)
                def _(step):
                    src = (sp + 1 + step) % n_sp
                    ref_copy(0, sp, local, src).wait_recv()
                    ref_copy(1, sp, local, src).wait_recv()

            lanes = pl.ds(pl.multiple_of(local * HEAD_DIM, HEAD_DIM), HEAD_DIM)
            blocks = [turn_of(turn + n) for n in range(at_once)]
            results = [attend(local, block) for block in blocks]
            for block, result in zip(blocks, results):
                o_buf[block, :, lanes] = result
            for block in blocks:
                @pl.when(block == sp)
                def _():
                    o_here(local).start()

                @pl.when(block != sp)
                def _(block=block):
                    o_copy(local, block, sp).start()

    @functools.partial(loop, chunks)
    def _(c):
        x_copy(c).wait_send()
        dest, local = head_of(c)

        @pl.when(dest != sp)
        def _():
            ref_copy(c, dest, local, sp).wait_send()

        for at in range(levels):
            @pl.when(level == at)
            def _(at=at):
                for way in (0, 1):
                    p = place(way, at)
                    if p < levels - 1:
                        for slot in range(slots_on(p, levels)):
                            line_copy(way, slot, c, x_buf.at[c], at).wait_send()

    @functools.partial(loop, n_sp - 1)
    def _(step):
        other = (sp + 1 + step) % n_sp
        for a in range(3):
            seq_copy(a, other, sp).wait_send()
        for local in range(per_dev):
            o_copy(local, other, sp).wait_send()
            o_copy(local, sp, other).wait_recv()

    for local in range(per_dev):
        o_here(local).wait()


def shards(n_grp, n_sp, queries, keys, values, ref_cache, ref_ids, ref_owner, ref_lens):
    tokens, width = queries.shape[1:]
    ref_tokens = ref_cache.shape[2]
    heads = width // HEAD_DIM
    chunks = 2 * heads
    per_dev = heads // n_sp
    feat = per_dev * HEAD_DIM
    levels = n_grp // PAIR
    slots = max(slots_on(p, levels) for p in range(levels - 1))
    chunk = (ref_tokens, HEAD_DIM)
    bf16 = jnp.bfloat16
    dma = pltpu.SemaphoreType.DMA
    smem = pl.BlockSpec(memory_space=pltpu.SMEM)
    hbm = pl.BlockSpec(memory_space=pl.ANY)
    all_keys = n_sp * (tokens + ref_tokens)
    return pl.pallas_call(
        functools.partial(kernel, n_grp, n_sp),
        out_shape=jax.ShapeDtypeStruct(queries.shape, bf16),
        in_specs=[smem] * 3 + [hbm] * 4,
        out_specs=hbm,
        scratch_shapes=[
            pltpu.VMEM((n_sp, tokens, feat), bf16),
            pltpu.VMEM((n_sp, tokens, feat), bf16),
            pltpu.VMEM((n_sp, tokens, feat), bf16),
            pltpu.VMEM((n_sp, tokens, feat), bf16),
            pltpu.VMEM((n_sp, tokens, feat), bf16),
            pltpu.VMEM((n_sp, tokens, feat), bf16),
            pltpu.VMEM((chunks,) + chunk, bf16),
            pltpu.VMEM((chunks,) + chunk, bf16),
            pltpu.VMEM((2, slots, chunks) + chunk, bf16),
            pltpu.VMEM((2, slots, chunks) + chunk, bf16),
            pltpu.VMEM((chunks,) + chunk, bf16),
            pltpu.VMEM((per_dev, 2, n_sp) + chunk, bf16),
            pltpu.VMEM((n_sp, tokens, feat), bf16),
            dma((chunks,)),
            dma((3,)),
            dma((3, n_sp)),
            dma((3, n_sp)),
            dma((3, n_sp)),
            dma((chunks,)),
            dma((chunks,)),
            dma((2, slots, chunks)),
            dma((2, slots, chunks)),
            dma((chunks,)),
            dma((per_dev, 2, n_sp)),
            dma((per_dev,)),
            dma((per_dev, n_sp)),
            dma((per_dev, n_sp)),
        ],
        compiler_params=pltpu.CompilerParams(
            collective_id=0, has_side_effects=True, vmem_limit_bytes=60 * 1024 * 1024
        ),
        cost_estimate=pl.CostEstimate(
            flops=4 * n_sp * tokens * all_keys * feat,
            bytes_accessed=8 * tokens * width * 2,
            transcendentals=per_dev * n_sp * tokens * all_keys,
        ),
    )(ref_ids, ref_owner, ref_lens, queries, keys, values, ref_cache)


def solution(mesh):
    in_specs = (
        P("grp", "sp", None),
        P("grp", "sp", None),
        P("grp", "sp", None),
        P("grp", None, "sp", None),
        P(),
        P(),
        P(),
    )
    body = functools.partial(shards, mesh.shape["grp"], mesh.shape["sp"])
    return jax.shard_map(
        body, mesh=mesh, in_specs=in_specs, out_specs=P("grp", "sp", None), check_vma=False
    )
```

```python
import functools
import math

import jax
import jax.numpy as jnp
from jax import lax
from jax.experimental import pallas as pl
from jax.experimental.pallas import tpu as pltpu
from jax.sharding import PartitionSpec as P

HEAD_DIM = 128
PAIR = 2
MESH = pl.DeviceIdType.MESH


def slots_on(p, levels):
    return min(PAIR * (p + 1), levels - 1 - p)


def sends_rows(p, levels):
    return PAIR * (p + 1) <= levels - 1 - p


def pick(options):
    value = options[-1][1]
    for cond, other in reversed(options[:-1]):
        value = lax.select(cond, other, value)
    return value


def kernel(
    n_grp, n_sp,
    ids_ref, owner_ref, lens_ref, q_hbm, k_hbm, v_hbm, ref_hbm, out_hbm,
    q_buf, k_buf, v_buf, q_stage, k_stage, v_stage, own_buf, x_buf, line_in, line_out, routed, ref_kv, o_buf,
    own_sem, keep_sem, stage_sem, seq_send, seq_recv, x_send, x_recv, line_send, line_recv,
    ref_send, ref_recv, o_keep, o_send, o_recv,
):
    levels = n_grp // PAIR
    heads = ref_hbm.shape[-1] // HEAD_DIM
    per_dev = heads // n_sp
    feat = per_dev * HEAD_DIM
    tokens = q_hbm.shape[1]
    ref_tokens = ref_hbm.shape[2]
    grp = lax.axis_index("grp")
    sp = lax.axis_index("sp")
    level = grp // PAIR
    side = grp % PAIR
    mate = level * PAIR + (1 - side)

    def at_level(other):
        return (other * PAIR + side, sp)

    def head_of(c):
        return (c + sp) % n_sp, c // n_sp

    def lanes_of(c):
        dest, local = head_of(c)
        return pl.ds(pl.multiple_of((dest * per_dev + local) * HEAD_DIM, HEAD_DIM), HEAD_DIM)

    def turn_of(step):
        return (sp // 2 * 2 + 2 + step) % n_sp

    def own_copy(c):
        return pltpu.make_async_copy(
            ref_hbm.at[0, :, :, lanes_of(c)], own_buf.at[c], own_sem.at[c]
        )

    def x_copy(c):
        return pltpu.make_async_remote_copy(
            src_ref=own_buf.at[c], dst_ref=x_buf.at[c],
            send_sem=x_send.at[c], recv_sem=x_recv.at[c],
            device_id=(mate, sp), device_id_type=MESH,
        )

    def line_copy(way, slot, c, src, other):
        return pltpu.make_async_remote_copy(
            src_ref=src, dst_ref=line_in.at[way, slot, c],
            send_sem=line_send.at[way, slot, c], recv_sem=line_recv.at[way, slot, c],
            device_id=at_level(other), device_id_type=MESH,
        )

    def ref_copy(c, dest, local, src):
        return pltpu.make_async_remote_copy(
            src_ref=routed.at[c], dst_ref=ref_kv.at[local, src],
            send_sem=ref_send.at[c], recv_sem=ref_recv.at[local, src],
            device_id=(grp, dest), device_id_type=MESH,
        )

    seq_refs = (
        (q_hbm, q_stage, q_buf), (k_hbm, k_stage, k_buf), (v_hbm, v_stage, v_buf)
    )

    def seq_lanes(dest):
        return pl.ds(pl.multiple_of(dest * feat, HEAD_DIM), feat)

    def seq_copy(a, dest, src):
        _, stage, buf = seq_refs[a]
        return pltpu.make_async_remote_copy(
            src_ref=stage.at[dest], dst_ref=buf.at[src],
            send_sem=seq_send.at[a, dest], recv_sem=seq_recv.at[a, src],
            device_id=(grp, dest), device_id_type=MESH,
        )

    def keep_copy(a):
        hbm, _, buf = seq_refs[a]
        return pltpu.make_async_copy(
            hbm.at[0, :, seq_lanes(sp)], buf.at[sp], keep_sem.at[a]
        )

    def stage_copy(a, dest):
        hbm, stage, _ = seq_refs[a]
        return pltpu.make_async_copy(
            hbm.at[0, :, seq_lanes(dest)], stage.at[dest], stage_sem.at[a, dest]
        )

    def o_copy(local, dest, src):
        lanes = pl.ds(pl.multiple_of(local * HEAD_DIM, HEAD_DIM), HEAD_DIM)
        out_lanes = pl.ds(pl.multiple_of(src * feat + local * HEAD_DIM, HEAD_DIM), HEAD_DIM)
        return pltpu.make_async_remote_copy(
            src_ref=o_buf.at[dest, :, lanes], dst_ref=out_hbm.at[0, :, out_lanes],
            send_sem=o_send.at[local, dest], recv_sem=o_recv.at[local, src],
            device_id=(grp, dest), device_id_type=MESH,
        )

    def o_here(local):
        lanes = pl.ds(pl.multiple_of(local * HEAD_DIM, HEAD_DIM), HEAD_DIM)
        out_lanes = pl.ds(pl.multiple_of(sp * feat + local * HEAD_DIM, HEAD_DIM), HEAD_DIM)
        return pltpu.make_async_copy(
            o_buf.at[sp, :, lanes], out_hbm.at[0, :, out_lanes], o_keep.at[local]
        )

    def loop(count, body):
        def step(i, carry):
            body(i)
            return carry
        lax.fori_loop(0, count, step, 0)

    x_ahead, ends_ahead = 8, 6
    seq_copies = 3 * (n_sp - 1)
    per_step = -(-seq_copies // 9)

    inner = jnp.logical_and(level > 0, level < levels - 1)

    @functools.partial(loop, heads)
    def _(c):
        own_copy(c).start()

    @functools.partial(loop, n_sp - 1)
    def _(step):
        for a in range(3):
            stage_copy(a, (sp + 1 + step) % n_sp).start()

    for a in range(3):
        keep_copy(a).start()

    barrier = pltpu.get_barrier_semaphore()

    def greet(device):
        pl.semaphore_signal(barrier, inc=1, device_id=device, device_id_type=MESH)

    greet((mate, sp))
    for step in range(1, n_sp):
        greet((grp, (sp + step) % n_sp))

    @pl.when(level > 0)
    def _():
        greet(at_level(level - 1))

    @pl.when(level < levels - 1)
    def _():
        greet(at_level(level + 1))

    pl.semaphore_wait(barrier, n_sp + 1 + inner.astype(jnp.int32))

    @functools.partial(loop, heads)
    def _(c):
        own_copy(c).wait()

    @functools.partial(loop, x_ahead)
    def _(c):
        x_copy(c).start()

    wanted = [owner_ref[ids_ref[lev * PAIR + side]] for lev in range(levels)]
    here = ids_ref[grp]
    my_row = owner_ref[here]
    live = lens_ref[here]

    def level_rows(c):
        own, other = own_buf[c], x_buf[c]
        return [lax.select(side == k, own, other) for k in range(PAIR)]

    def send_own(at, c):
        way, ahead = (0, at + 1) if at == 0 else (1, at - 1)
        line_copy(way, side, c, own_buf.at[c], ahead).start()

    def send_other(at, c):
        way, ahead = (0, at + 1) if at == 0 else (1, at - 1)
        x_copy(c).wait_recv()
        line_copy(way, 1 - side, c, x_buf.at[c], ahead).start()

    for at in (0, levels - 1):
        @pl.when(level == at)
        def _(at=at):
            send_own(at, 0)

            @functools.partial(loop, ends_ahead)
            def _(c):
                send_other(at, c)
                send_own(at, c + 1)

    def place(way, lev):
        return lev if way == 0 else levels - 1 - lev

    def relay(at, way, c):
        p = place(way, at)
        ahead = at + 1 if way == 0 else at - 1
        for slot in range(slots_on(p - 1, levels)):
            line_copy(way, slot, c, x_buf.at[c], at).wait_recv()
        if p == levels - 1:
            return
        count = slots_on(p, levels)
        if sends_rows(p, levels):
            for slot in range(PAIR * p):
                line_copy(way, slot, c, line_in.at[way, slot, c], ahead).start()
            line_copy(way, PAIR * p + side, c, own_buf.at[c], ahead).start()
            line_copy(way, PAIR * p + 1 - side, c, x_buf.at[c], ahead).start()
            return
        rows = level_rows(c)
        for slot in range(count):
            row = wanted[place(way, p + 1 + slot)]
            value = pick(line_options(at, way, c, row, slot + 1, rows))
            line_out[way, slot, c] = value
            line_copy(way, slot, c, line_out.at[way, slot, c], ahead).start()

    def line_options(at, way, c, row, slot, rows):
        p = place(way, at)
        options = [(row == at * PAIR + k, rows[k]) for k in range(PAIR)]
        if p == 0:
            return options
        if sends_rows(p - 1, levels):
            return options + [
                (row == place(way, q) * PAIR + k, line_in[way, PAIR * q + k, c])
                for q in range(p) for k in range(PAIR)
            ]
        return options + [(row // PAIR < at if way == 0 else row // PAIR > at, line_in[way, slot, c])]

    def final(at, c):
        rows = level_rows(c)
        options = line_options(at, 0, c, my_row, 0, rows)
        options = options + line_options(at, 1, c, my_row, 0, rows)[PAIR:]
        value = pick(options)
        dest, local = head_of(c)

        @pl.when(dest == sp)
        def _():
            ref_kv[local, sp] = value

        @pl.when(dest != sp)
        def _():
            routed[c] = value
            ref_copy(c, dest, local, sp).start()

    def attend(local, block):
        lanes = pl.ds(pl.multiple_of(local * HEAD_DIM, HEAD_DIM), HEAD_DIM)
        own_keys, ref_keys = n_sp * tokens, n_sp * ref_tokens
        q = q_buf[block, :, lanes]
        k = k_buf[:, :, lanes].reshape(own_keys, HEAD_DIM)
        v = v_buf[:, :, lanes].reshape(own_keys, HEAD_DIM)
        ref_k = ref_kv[local, :, 0].reshape(ref_keys, HEAD_DIM)
        ref_v = ref_kv[local, :, 1].reshape(ref_keys, HEAD_DIM)
        contract = (((1,), (1,)), ((), ()))
        scale = HEAD_DIM ** -0.5 * math.log2(math.e)
        s_own = lax.dot_general(q, k, contract, preferred_element_type=jnp.float32)
        s_ref = lax.dot_general(q, ref_k, contract, preferred_element_type=jnp.float32)
        col = lax.broadcasted_iota(jnp.int32, s_ref.shape, 1)
        s_ref = jnp.where(col < live, s_ref, -jnp.inf)
        peak = jnp.maximum(
            jnp.max(s_own, axis=1, keepdims=True), jnp.max(s_ref, axis=1, keepdims=True)
        )
        w_own = jnp.exp2((s_own - peak) * scale)
        w_ref = jnp.exp2((s_ref - peak) * scale)
        total = jnp.sum(w_own, axis=1, keepdims=True) + jnp.sum(w_ref, axis=1, keepdims=True)
        mixed = jnp.dot(w_own.astype(jnp.bfloat16), v, preferred_element_type=jnp.float32)
        mixed += jnp.dot(w_ref.astype(jnp.bfloat16), ref_v, preferred_element_type=jnp.float32)
        return (mixed / total).astype(jnp.bfloat16)

    last_lag = levels
    units = per_dev * n_sp
    at_once = 2
    per_head = n_sp // at_once
    last_start = heads - 1 + last_lag
    first_unit = max(
        [3 * heads // 4]
        + [(n + 1) * n_sp - 1 + last_lag - n * per_head for n in range(per_dev - 1)]
    )

    @functools.partial(loop, last_start + per_head)
    def _(i):
        @pl.when(i + x_ahead < heads)
        def _():
            x_copy(i + x_ahead).start()

        @pl.when(jnp.logical_and(inner, i < heads))
        def _():
            x_copy(i).wait_recv()

        for at in range(levels):
            @pl.when(level == at)
            def _(at=at):
                if at in (0, levels - 1):
                    @pl.when(i + ends_ahead < heads)
                    def _():
                        send_other(at, i + ends_ahead)

                    @pl.when(i + ends_ahead + 1 < heads)
                    def _():
                        send_own(at, i + ends_ahead + 1)

                for p, way in sorted((place(way, at), way) for way in (0, 1)):
                    if p == 0:
                        continue
                    c = i - (0 if p == 1 else p + 1)

                    @pl.when(jnp.logical_and(c >= 0, c < heads))
                    def _(c=c, way=way):
                        relay(at, way, c)

                done = i - last_lag

                @pl.when(jnp.logical_and(done >= 0, done < heads))
                def _():
                    final(at, done)

        for n in range(per_step):
            number = i * per_step + n

            @pl.when(number < seq_copies)
            def _(number=number):
                dest = (sp + 1 + number // 3) % n_sp
                for a in range(3):
                    @pl.when(number % 3 == a)
                    def _(a=a):
                        stage_copy(a, dest).wait()
                        seq_copy(a, dest, sp).start()

        early = (i - first_unit) * at_once
        late = (i - last_start) * at_once + units - n_sp
        unit = jnp.where(i >= last_start, late, early)
        due = jnp.logical_or(
            jnp.logical_and(early >= 0, early < units - n_sp), i >= last_start
        )

        @pl.when(due)
        def _():
            local, turn = unit // n_sp, unit % n_sp

            @pl.when(unit == 0)
            def _():
                for a in range(3):
                    keep_copy(a).wait()

                @functools.partial(loop, n_sp - 1)
                def _(step):
                    src = (sp + 1 + step) % n_sp
                    for a in range(3):
                        seq_copy(a, sp, src).wait_recv()

            @pl.when(turn == 0)
            def _():
                @functools.partial(loop, n_sp - 1)
                def _(step):
                    src = (sp + 1 + step) % n_sp
                    ref_copy(0, sp, local, src).wait_recv()

            lanes = pl.ds(pl.multiple_of(local * HEAD_DIM, HEAD_DIM), HEAD_DIM)
            blocks = [turn_of(turn + n) for n in range(at_once)]
            results = [attend(local, block) for block in blocks]
            for block, result in zip(blocks, results):
                o_buf[block, :, lanes] = result
            for block in blocks:
                @pl.when(block == sp)
                def _():
                    o_here(local).start()

                @pl.when(block != sp)
                def _(block=block):
                    o_copy(local, block, sp).start()

    @functools.partial(loop, heads)
    def _(c):
        x_copy(c).wait_send()
        dest, local = head_of(c)

        @pl.when(dest != sp)
        def _():
            ref_copy(c, dest, local, sp).wait_send()

        for at in range(levels):
            @pl.when(level == at)
            def _(at=at):
                for way in (0, 1):
                    p = place(way, at)
                    if p < levels - 1:
                        for slot in range(slots_on(p, levels)):
                            line_copy(way, slot, c, x_buf.at[c], at).wait_send()

    @functools.partial(loop, n_sp - 1)
    def _(step):
        other = (sp + 1 + step) % n_sp
        for a in range(3):
            seq_copy(a, other, sp).wait_send()
        for local in range(per_dev):
            o_copy(local, other, sp).wait_send()
            o_copy(local, sp, other).wait_recv()

    for local in range(per_dev):
        o_here(local).wait()


def shards(n_grp, n_sp, queries, keys, values, ref_cache, ref_ids, ref_owner, ref_lens):
    tokens, width = queries.shape[1:]
    ref_tokens = ref_cache.shape[2]
    heads = width // HEAD_DIM
    per_dev = heads // n_sp
    feat = per_dev * HEAD_DIM
    levels = n_grp // PAIR
    slots = max(slots_on(p, levels) for p in range(levels - 1))
    chunk = (2, ref_tokens, HEAD_DIM)
    bf16 = jnp.bfloat16
    dma = pltpu.SemaphoreType.DMA
    smem = pl.BlockSpec(memory_space=pltpu.SMEM)
    hbm = pl.BlockSpec(memory_space=pl.ANY)
    all_keys = n_sp * (tokens + ref_tokens)
    return pl.pallas_call(
        functools.partial(kernel, n_grp, n_sp),
        out_shape=jax.ShapeDtypeStruct(queries.shape, bf16),
        in_specs=[smem] * 3 + [hbm] * 4,
        out_specs=hbm,
        scratch_shapes=[
            pltpu.VMEM((n_sp, tokens, feat), bf16),
            pltpu.VMEM((n_sp, tokens, feat), bf16),
            pltpu.VMEM((n_sp, tokens, feat), bf16),
            pltpu.VMEM((n_sp, tokens, feat), bf16),
            pltpu.VMEM((n_sp, tokens, feat), bf16),
            pltpu.VMEM((n_sp, tokens, feat), bf16),
            pltpu.VMEM((heads,) + chunk, bf16),
            pltpu.VMEM((heads,) + chunk, bf16),
            pltpu.VMEM((2, slots, heads) + chunk, bf16),
            pltpu.VMEM((2, slots, heads) + chunk, bf16),
            pltpu.VMEM((heads,) + chunk, bf16),
            pltpu.VMEM((per_dev, n_sp) + chunk, bf16),
            pltpu.VMEM((n_sp, tokens, feat), bf16),
            dma((heads,)),
            dma((3,)),
            dma((3, n_sp)),
            dma((3, n_sp)),
            dma((3, n_sp)),
            dma((heads,)),
            dma((heads,)),
            dma((2, slots, heads)),
            dma((2, slots, heads)),
            dma((heads,)),
            dma((per_dev, n_sp)),
            dma((per_dev,)),
            dma((per_dev, n_sp)),
            dma((per_dev, n_sp)),
        ],
        compiler_params=pltpu.CompilerParams(
            collective_id=0, has_side_effects=True, vmem_limit_bytes=60 * 1024 * 1024
        ),
        cost_estimate=pl.CostEstimate(
            flops=4 * n_sp * tokens * all_keys * feat,
            bytes_accessed=8 * tokens * width * 2,
            transcendentals=per_dev * n_sp * tokens * all_keys,
        ),
    )(ref_ids, ref_owner, ref_lens, queries, keys, values, ref_cache)


def solution(mesh):
    in_specs = (
        P("grp", "sp", None),
        P("grp", "sp", None),
        P("grp", "sp", None),
        P("grp", None, "sp", None),
        P(),
        P(),
        P(),
    )
    body = functools.partial(shards, mesh.shape["grp"], mesh.shape["sp"])
    return jax.shard_map(
        body, mesh=mesh, in_specs=in_specs, out_specs=P("grp", "sp", None), check_vma=False
    )
```

```python
import functools
import math

import jax
import jax.numpy as jnp
from jax import lax
from jax.experimental import pallas as pl
from jax.experimental.pallas import tpu as pltpu
from jax.sharding import PartitionSpec as P

HEAD_DIM = 128
PAIR = 2
MESH = pl.DeviceIdType.MESH


def slots_on(p, levels):
    return min(PAIR * (p + 1), levels - 1 - p)


def sends_rows(p, levels):
    return PAIR * (p + 1) <= levels - 1 - p


def pick(options):
    value = options[-1][1]
    for cond, other in reversed(options[:-1]):
        value = lax.select(cond, other, value)
    return value


def kernel(
    n_grp, n_sp,
    ids_ref, owner_ref, lens_ref, q_hbm, k_hbm, v_hbm, ref_hbm, out_hbm,
    q_buf, k_buf, v_buf, q_stage, k_stage, v_stage, own_buf, x_buf, line_in, line_out, routed, ref_kv, o_buf,
    own_sem, keep_sem, stage_sem, seq_send, seq_recv, x_send, x_recv, line_send, line_recv,
    ref_send, ref_recv, o_keep, o_send, o_recv,
):
    levels = n_grp // PAIR
    heads = ref_hbm.shape[-1] // HEAD_DIM
    per_dev = heads // n_sp
    feat = per_dev * HEAD_DIM
    tokens = q_hbm.shape[1]
    ref_tokens = ref_hbm.shape[2]
    grp = lax.axis_index("grp")
    sp = lax.axis_index("sp")
    level = grp // PAIR
    side = grp % PAIR
    mate = level * PAIR + (1 - side)

    def at_level(other):
        return (other * PAIR + side, sp)

    def head_of(c):
        return (c + sp) % n_sp, c // n_sp

    def lanes_of(c):
        dest, local = head_of(c)
        return pl.ds(pl.multiple_of((dest * per_dev + local) * HEAD_DIM, HEAD_DIM), HEAD_DIM)

    def turn_of(step):
        return (sp // 2 * 2 + 2 + step) % n_sp

    def own_copy(c):
        return pltpu.make_async_copy(
            ref_hbm.at[0, :, :, lanes_of(c)], own_buf.at[c], own_sem.at[c]
        )

    def x_copy(c):
        return pltpu.make_async_remote_copy(
            src_ref=own_buf.at[c], dst_ref=x_buf.at[c],
            send_sem=x_send.at[c], recv_sem=x_recv.at[c],
            device_id=(mate, sp), device_id_type=MESH,
        )

    def line_copy(way, slot, c, src, other):
        return pltpu.make_async_remote_copy(
            src_ref=src, dst_ref=line_in.at[way, slot, c],
            send_sem=line_send.at[way, slot, c], recv_sem=line_recv.at[way, slot, c],
            device_id=at_level(other), device_id_type=MESH,
        )

    def ref_copy(c, dest, local, src):
        return pltpu.make_async_remote_copy(
            src_ref=routed.at[c], dst_ref=ref_kv.at[local, src],
            send_sem=ref_send.at[c], recv_sem=ref_recv.at[local, src],
            device_id=(grp, dest), device_id_type=MESH,
        )

    seq_refs = (
        (q_hbm, q_stage, q_buf), (k_hbm, k_stage, k_buf), (v_hbm, v_stage, v_buf)
    )

    def seq_lanes(dest):
        return pl.ds(pl.multiple_of(dest * feat, HEAD_DIM), feat)

    def seq_copy(a, dest, src):
        _, stage, buf = seq_refs[a]
        return pltpu.make_async_remote_copy(
            src_ref=stage.at[dest], dst_ref=buf.at[src],
            send_sem=seq_send.at[a, dest], recv_sem=seq_recv.at[a, src],
            device_id=(grp, dest), device_id_type=MESH,
        )

    def keep_copy(a):
        hbm, _, buf = seq_refs[a]
        return pltpu.make_async_copy(
            hbm.at[0, :, seq_lanes(sp)], buf.at[sp], keep_sem.at[a]
        )

    def stage_copy(a, dest):
        hbm, stage, _ = seq_refs[a]
        return pltpu.make_async_copy(
            hbm.at[0, :, seq_lanes(dest)], stage.at[dest], stage_sem.at[a, dest]
        )

    def o_copy(local, dest, src):
        lanes = pl.ds(pl.multiple_of(local * HEAD_DIM, HEAD_DIM), HEAD_DIM)
        out_lanes = pl.ds(pl.multiple_of(src * feat + local * HEAD_DIM, HEAD_DIM), HEAD_DIM)
        return pltpu.make_async_remote_copy(
            src_ref=o_buf.at[dest, :, lanes], dst_ref=out_hbm.at[0, :, out_lanes],
            send_sem=o_send.at[local, dest], recv_sem=o_recv.at[local, src],
            device_id=(grp, dest), device_id_type=MESH,
        )

    def o_here(local):
        lanes = pl.ds(pl.multiple_of(local * HEAD_DIM, HEAD_DIM), HEAD_DIM)
        out_lanes = pl.ds(pl.multiple_of(sp * feat + local * HEAD_DIM, HEAD_DIM), HEAD_DIM)
        return pltpu.make_async_copy(
            o_buf.at[sp, :, lanes], out_hbm.at[0, :, out_lanes], o_keep.at[local]
        )

    def loop(count, body):
        def step(i, carry):
            body(i)
            return carry
        lax.fori_loop(0, count, step, 0)

    x_ahead, ends_ahead = 8, 6
    seq_copies = 3 * (n_sp - 1)
    per_step = -(-seq_copies // 9)

    inner = jnp.logical_and(level > 0, level < levels - 1)

    @functools.partial(loop, heads)
    def _(c):
        own_copy(c).start()

    @functools.partial(loop, n_sp - 1)
    def _(step):
        for a in range(3):
            stage_copy(a, (sp + 1 + step) % n_sp).start()

    for a in range(3):
        keep_copy(a).start()

    barrier = pltpu.get_barrier_semaphore()

    def greet(device):
        pl.semaphore_signal(barrier, inc=1, device_id=device, device_id_type=MESH)

    greet((mate, sp))
    for step in range(1, n_sp):
        greet((grp, (sp + step) % n_sp))

    @pl.when(level > 0)
    def _():
        greet(at_level(level - 1))

    @pl.when(level < levels - 1)
    def _():
        greet(at_level(level + 1))

    pl.semaphore_wait(barrier, n_sp + 1 + inner.astype(jnp.int32))

    @functools.partial(loop, heads)
    def _(c):
        own_copy(c).wait()

    @functools.partial(loop, x_ahead)
    def _(c):
        x_copy(c).start()

    wanted = [owner_ref[ids_ref[lev * PAIR + side]] for lev in range(levels)]
    here = ids_ref[grp]
    my_row = owner_ref[here]
    live = lens_ref[here]

    def level_rows(c):
        own, other = own_buf[c], x_buf[c]
        return [lax.select(side == k, own, other) for k in range(PAIR)]

    def send_own(at, c):
        way, ahead = (0, at + 1) if at == 0 else (1, at - 1)
        line_copy(way, side, c, own_buf.at[c], ahead).start()

    def send_other(at, c):
        way, ahead = (0, at + 1) if at == 0 else (1, at - 1)
        x_copy(c).wait_recv()
        line_copy(way, 1 - side, c, x_buf.at[c], ahead).start()

    for at in (0, levels - 1):
        @pl.when(level == at)
        def _(at=at):
            send_own(at, 0)

            @functools.partial(loop, ends_ahead)
            def _(c):
                send_other(at, c)
                send_own(at, c + 1)

    def place(way, lev):
        return lev if way == 0 else levels - 1 - lev

    def relay(at, way, c):
        p = place(way, at)
        ahead = at + 1 if way == 0 else at - 1
        for slot in range(slots_on(p - 1, levels)):
            line_copy(way, slot, c, x_buf.at[c], at).wait_recv()
        if p == levels - 1:
            return
        count = slots_on(p, levels)
        if sends_rows(p, levels):
            for slot in range(PAIR * p):
                line_copy(way, slot, c, line_in.at[way, slot, c], ahead).start()
            line_copy(way, PAIR * p + side, c, own_buf.at[c], ahead).start()
            line_copy(way, PAIR * p + 1 - side, c, x_buf.at[c], ahead).start()
            return
        rows = level_rows(c)
        for slot in range(count):
            row = wanted[place(way, p + 1 + slot)]
            value = pick(line_options(at, way, c, row, slot + 1, rows))
            line_out[way, slot, c] = value
            line_copy(way, slot, c, line_out.at[way, slot, c], ahead).start()

    def line_options(at, way, c, row, slot, rows):
        p = place(way, at)
        options = [(row == at * PAIR + k, rows[k]) for k in range(PAIR)]
        if p == 0:
            return options
        if sends_rows(p - 1, levels):
            return options + [
                (row == place(way, q) * PAIR + k, line_in[way, PAIR * q + k, c])
                for q in range(p) for k in range(PAIR)
            ]
        return options + [(row // PAIR < at if way == 0 else row // PAIR > at, line_in[way, slot, c])]

    def final(at, c):
        rows = level_rows(c)
        options = line_options(at, 0, c, my_row, 0, rows)
        options = options + line_options(at, 1, c, my_row, 0, rows)[PAIR:]
        value = pick(options)
        dest, local = head_of(c)

        @pl.when(dest == sp)
        def _():
            ref_kv[local, sp] = value

        @pl.when(dest != sp)
        def _():
            routed[c] = value
            ref_copy(c, dest, local, sp).start()

    def attend(local, block):
        lanes = pl.ds(pl.multiple_of(local * HEAD_DIM, HEAD_DIM), HEAD_DIM)
        own_keys, ref_keys = n_sp * tokens, n_sp * ref_tokens
        q = q_buf[block, :, lanes]
        k = k_buf[:, :, lanes].reshape(own_keys, HEAD_DIM)
        v = v_buf[:, :, lanes].reshape(own_keys, HEAD_DIM)
        ref_k = ref_kv[local, :, 0].reshape(ref_keys, HEAD_DIM)
        ref_v = ref_kv[local, :, 1].reshape(ref_keys, HEAD_DIM)
        contract = (((1,), (1,)), ((), ()))
        scale = HEAD_DIM ** -0.5 * math.log2(math.e)
        s_own = lax.dot_general(q, k, contract, preferred_element_type=jnp.float32)
        s_ref = lax.dot_general(q, ref_k, contract, preferred_element_type=jnp.float32)
        col = lax.broadcasted_iota(jnp.int32, s_ref.shape, 1)
        s_ref = jnp.where(col < live, s_ref, -jnp.inf)
        peak = jnp.maximum(
            jnp.max(s_own, axis=1, keepdims=True), jnp.max(s_ref, axis=1, keepdims=True)
        )
        w_own = jnp.exp2((s_own - peak) * scale)
        w_ref = jnp.exp2((s_ref - peak) * scale)
        total = jnp.sum(w_own, axis=1, keepdims=True) + jnp.sum(w_ref, axis=1, keepdims=True)
        mixed = jnp.dot(w_own.astype(jnp.bfloat16), v, preferred_element_type=jnp.float32)
        mixed += jnp.dot(w_ref.astype(jnp.bfloat16), ref_v, preferred_element_type=jnp.float32)
        return (mixed / total).astype(jnp.bfloat16)

    last_lag = levels
    units = per_dev * n_sp
    at_once = 2
    per_head = n_sp // at_once
    last_start = heads - 1 + last_lag
    first_unit = max(
        [3 * heads // 4]
        + [(n + 1) * n_sp - 1 + last_lag - n * per_head for n in range(per_dev - 1)]
    )

    @functools.partial(loop, last_start + per_head)
    def _(i):
        @pl.when(i + x_ahead < heads)
        def _():
            x_copy(i + x_ahead).start()

        @pl.when(jnp.logical_and(inner, i < heads))
        def _():
            x_copy(i).wait_recv()

        for at in range(levels):
            @pl.when(level == at)
            def _(at=at):
                if at in (0, levels - 1):
                    @pl.when(i + ends_ahead < heads)
                    def _():
                        send_other(at, i + ends_ahead)

                    @pl.when(i + ends_ahead + 1 < heads)
                    def _():
                        send_own(at, i + ends_ahead + 1)

                for p, way in sorted((place(way, at), way) for way in (0, 1)):
                    if p == 0:
                        continue
                    c = i - (0 if p == 1 else p + 1)

                    @pl.when(jnp.logical_and(c >= 0, c < heads))
                    def _(c=c, way=way):
                        relay(at, way, c)

                done = i - last_lag

                @pl.when(jnp.logical_and(done >= 0, done < heads))
                def _():
                    final(at, done)

        for n in range(per_step):
            number = i * per_step + n

            @pl.when(number < seq_copies)
            def _(number=number):
                dest = (sp + 1 + number // 3) % n_sp
                for a in range(3):
                    @pl.when(number % 3 == a)
                    def _(a=a):
                        stage_copy(a, dest).wait()
                        seq_copy(a, dest, sp).start()

        early = (i - first_unit) * at_once
        late = (i - last_start) * at_once + units - n_sp
        unit = jnp.where(i >= last_start, late, early)
        due = jnp.logical_or(
            jnp.logical_and(early >= 0, early < units - n_sp), i >= last_start
        )

        @pl.when(due)
        def _():
            local, turn = unit // n_sp, unit % n_sp

            @pl.when(unit == 0)
            def _():
                for a in range(3):
                    keep_copy(a).wait()

                @functools.partial(loop, n_sp - 1)
                def _(step):
                    src = (sp + 1 + step) % n_sp
                    for a in range(3):
                        seq_copy(a, sp, src).wait_recv()

            @pl.when(turn == 0)
            def _():
                @functools.partial(loop, n_sp - 1)
                def _(step):
                    src = (sp + 1 + step) % n_sp
                    ref_copy(0, sp, local, src).wait_recv()

            lanes = pl.ds(pl.multiple_of(local * HEAD_DIM, HEAD_DIM), HEAD_DIM)
            blocks = [turn_of(turn + n) for n in range(at_once)]
            results = [attend(local, block) for block in blocks]
            for block, result in zip(blocks, results):
                o_buf[block, :, lanes] = result
            for block in blocks:
                @pl.when(block == sp)
                def _():
                    o_here(local).start()

                @pl.when(block != sp)
                def _(block=block):
                    o_copy(local, block, sp).start()

    @functools.partial(loop, heads)
    def _(c):
        x_copy(c).wait_send()
        dest, local = head_of(c)

        @pl.when(dest != sp)
        def _():
            ref_copy(c, dest, local, sp).wait_send()

        for at in range(levels):
            @pl.when(level == at)
            def _(at=at):
                for way in (0, 1):
                    p = place(way, at)
                    if p < levels - 1:
                        for slot in range(slots_on(p, levels)):
                            line_copy(way, slot, c, x_buf.at[c], at).wait_send()

    @functools.partial(loop, n_sp - 1)
    def _(step):
        other = (sp + 1 + step) % n_sp
        for a in range(3):
            seq_copy(a, other, sp).wait_send()
        for local in range(per_dev):
            o_copy(local, other, sp).wait_send()
            o_copy(local, sp, other).wait_recv()

    for local in range(per_dev):
        o_here(local).wait()


def hand_over(src, dst, sems):
    pieces = sems.shape[0]
    rows = src.shape[1] // pieces
    copies = [
        pltpu.make_async_copy(
            src.at[:, n * rows:(n + 1) * rows], dst.at[:, n * rows:(n + 1) * rows], sems.at[n]
        )
        for n in range(pieces)
    ]
    for copy in copies:
        copy.start()
    for copy in copies:
        copy.wait()


def shards(n_grp, n_sp, queries, keys, values, ref_cache, ref_ids, ref_owner, ref_lens):
    tokens, width = queries.shape[1:]
    ref_tokens = ref_cache.shape[2]
    heads = width // HEAD_DIM
    per_dev = heads // n_sp
    feat = per_dev * HEAD_DIM
    levels = n_grp // PAIR
    slots = max(slots_on(p, levels) for p in range(levels - 1))
    chunk = (2, ref_tokens, HEAD_DIM)
    bf16 = jnp.bfloat16
    dma = pltpu.SemaphoreType.DMA
    smem = pl.BlockSpec(memory_space=pltpu.SMEM)
    hbm = pl.BlockSpec(memory_space=pl.ANY)
    all_keys = n_sp * (tokens + ref_tokens)
    attended = pl.pallas_call(
        functools.partial(kernel, n_grp, n_sp),
        out_shape=jax.ShapeDtypeStruct(queries.shape, bf16),
        in_specs=[smem] * 3 + [hbm] * 4,
        out_specs=hbm,
        scratch_shapes=[
            pltpu.VMEM((n_sp, tokens, feat), bf16),
            pltpu.VMEM((n_sp, tokens, feat), bf16),
            pltpu.VMEM((n_sp, tokens, feat), bf16),
            pltpu.VMEM((n_sp, tokens, feat), bf16),
            pltpu.VMEM((n_sp, tokens, feat), bf16),
            pltpu.VMEM((n_sp, tokens, feat), bf16),
            pltpu.VMEM((heads,) + chunk, bf16),
            pltpu.VMEM((heads,) + chunk, bf16),
            pltpu.VMEM((2, slots, heads) + chunk, bf16),
            pltpu.VMEM((2, slots, heads) + chunk, bf16),
            pltpu.VMEM((heads,) + chunk, bf16),
            pltpu.VMEM((per_dev, n_sp) + chunk, bf16),
            pltpu.VMEM((n_sp, tokens, feat), bf16),
            dma((heads,)),
            dma((3,)),
            dma((3, n_sp)),
            dma((3, n_sp)),
            dma((3, n_sp)),
            dma((heads,)),
            dma((heads,)),
            dma((2, slots, heads)),
            dma((2, slots, heads)),
            dma((heads,)),
            dma((per_dev, n_sp)),
            dma((per_dev,)),
            dma((per_dev, n_sp)),
            dma((per_dev, n_sp)),
        ],
        compiler_params=pltpu.CompilerParams(
            collective_id=0, has_side_effects=True, vmem_limit_bytes=60 * 1024 * 1024
        ),
        cost_estimate=pl.CostEstimate(
            flops=4 * n_sp * tokens * all_keys * feat,
            bytes_accessed=8 * tokens * width * 2,
            transcendentals=per_dev * n_sp * tokens * all_keys,
        ),
    )(ref_ids, ref_owner, ref_lens, queries, keys, values, ref_cache)
    return pl.pallas_call(
        hand_over,
        out_shape=jax.ShapeDtypeStruct(queries.shape, bf16),
        in_specs=[hbm],
        out_specs=hbm,
        scratch_shapes=[dma((4,))],
    )(attended)


def solution(mesh):
    in_specs = (
        P("grp", "sp", None),
        P("grp", "sp", None),
        P("grp", "sp", None),
        P("grp", None, "sp", None),
        P(),
        P(),
        P(),
    )
    body = functools.partial(shards, mesh.shape["grp"], mesh.shape["sp"])
    return jax.shard_map(
        body, mesh=mesh, in_specs=in_specs, out_specs=P("grp", "sp", None), check_vma=False
    )
```
